32 devices in a mesh: view: 4 (over y, core), row: 4 (over z), col: 2 (over x).
Axes of the slice: x: 2, y: 2, z: 4, core: 2. Of those that a mesh axis runs over, the one named last changes fastest.
Arguments:
- view_maps: bfloat16 [16, 16, 32, 768], P('view', 'row', 'col'), may hold values from -6 to 6
- gain_spatial: float32 [768], replicated, may hold values from 0.1 to 1.9
- spatial_query: bfloat16 [768, 768], replicated, may hold values from -8 to 8
- spatial_key: bfloat16 [768, 768], replicated, may hold values from -8 to 8
- spatial_value: bfloat16 [768, 768], replicated, may hold values from -0.21875 to 0.21875
- spatial_output: bfloat16 [768, 768], replicated, may hold values from -0.21875 to 0.21875
- gain_temporal: float32 [768], replicated, may hold values from 0.1 to 1.9
- temporal_query: bfloat16 [768, 768], replicated, may hold values from -8 to 8
- temporal_key: bfloat16 [768, 768], replicated, may hold values from -8 to 8
- temporal_value: bfloat16 [768, 768], replicated, may hold values from -0.21875 to 0.21875
- temporal_output: bfloat16 [768, 768], replicated, may hold values from -0.21875 to 0.21875
Outputs:
- refined: bfloat16 [16, 16, 32, 768], P('view', 'row', 'col')
The draws below stay inside these ranges and needn't reach their ends.
All inputs are finite; a program needn't handle non-finite values.
Results may differ from the reference program's by a relative error of at most 0.012.
Values may be sent and summed in bfloat16 or wider, within the bound.
A program may use at most 64 MiB of HBM per device.

```python
import jax
import jax.numpy as jnp
from jax import lax

D = 768
HEADS = 12
HEAD_DIM = 64
RADIUS = 3
VIEWS = 16
MAP_H = 16
MAP_W = 32


def paired_weights(key, which):
    base = jax.random.fold_in(key, 100 + which)
    first = jax.random.normal(jax.random.fold_in(base, 1), (D, D), jnp.float32) * D ** (-0.5)
    second = jax.random.normal(jax.random.fold_in(base, 2), (D, D), jnp.float32) * D ** (-0.5)
    first = jnp.clip(first, -8.0, 8.0)
    second = jnp.clip(second, -8.0, 8.0)
    return (first.astype(jnp.bfloat16), second.astype(jnp.bfloat16))


def draw_spatial_query(key, part):
    return paired_weights(key, 0)[0]


def draw_spatial_key(key, part):
    return paired_weights(key, 0)[1]


def draw_temporal_query(key, part):
    return paired_weights(key, 1)[0]


def draw_temporal_key(key, part):
    return paired_weights(key, 1)[1]


def block_levels(own_key, extent, cuts, least, largest):
    gain, own = 1.0, jax.random.fold_in(own_key, 6)
    for dim, blocks in cuts:
        heights = jnp.exp(jax.random.uniform(jax.random.fold_in(own, dim), (blocks,), jnp.float32, least / len(cuts), largest / len(cuts)))
        gain = gain * jnp.repeat(heights, extent[dim] // blocks).reshape([-1 if axis == dim else 1 for axis in range(len(extent))])
    return gain


def noise(stream_key, extent, scale, bound, cuts=(), held_as=jnp.bfloat16):
    level = block_levels(stream_key, extent, cuts, -0.22, 0.18) if cuts else 1.0
    values = jax.random.normal(stream_key, extent, jnp.float32) * scale * level
    return jnp.minimum(jnp.maximum(values, -bound), bound).astype(held_as)


def setup_inputs(seed: int = 0) -> dict:
    splits = jax.random.split(jax.random.key(seed), 12)
    view_maps = noise(splits[0], (VIEWS, MAP_H, MAP_W, D), 1.0, 6.0, ((0, 4), (1, 4), (2, 2)))
    gain_spatial = jnp.clip(1.0 + 0.18 * jax.random.normal(splits[1], (D,), jnp.float32), 0.1, 1.9)
    spatial_query = draw_spatial_query(jax.random.fold_in(splits[11], 71), 0)
    spatial_key = draw_spatial_key(jax.random.fold_in(splits[11], 71), 0)
    spatial_value = noise(splits[4], (D, D), D ** -0.5, 0.21875)
    spatial_output = noise(splits[5], (D, D), D ** -0.5, 0.21875)
    gain_temporal = jnp.clip(1.0 + 0.18 * jax.random.normal(splits[6], (D,), jnp.float32), 0.1, 1.9)
    temporal_query = draw_temporal_query(jax.random.fold_in(splits[11], 71), 0)
    temporal_key = draw_temporal_key(jax.random.fold_in(splits[11], 71), 0)
    temporal_value = noise(splits[9], (D, D), D ** -0.5, 0.21875)
    temporal_output = noise(splits[10], (D, D), D ** -0.5, 0.21875)
    return dict(view_maps=view_maps, gain_spatial=gain_spatial, spatial_query=spatial_query, spatial_key=spatial_key, spatial_value=spatial_value, spatial_output=spatial_output, gain_temporal=gain_temporal, temporal_query=temporal_query, temporal_key=temporal_key, temporal_value=temporal_value, temporal_output=temporal_output)


epsilon = 1e-06
very_negative = -1e+30

def rms_norm(tokens, gain_vector):
    values = tokens.astype(jnp.float32)
    scaled = values * lax.rsqrt(lax.optimization_barrier(jnp.mean(values * values, axis=-1, keepdims=True)) + epsilon)
    return (scaled * gain_vector).astype(jnp.bfloat16)

def project(tokens, weight_matrix):
    flat = tokens.reshape(-1, tokens.shape[-1])
    result = jnp.dot(flat, weight_matrix, preferred_element_type=jnp.float32)
    return result.reshape(tokens.shape[:-1] + (weight_matrix.shape[1],))

def neighbour(queries, keys_wide, values_wide, row_places, col_places, total_rows, total_cols):
    height, width = (queries.shape[1], queries.shape[2])
    head_shape = queries.shape[:-1] + (HEADS, HEAD_DIM)
    query_float = queries.astype(jnp.float32).reshape(head_shape)
    factor = HEAD_DIM ** (-0.5)
    score_list = []
    valid_list = []
    span = 2 * RADIUS + 1
    for offset_row in range(span):
        for offset_col in range(span):
            shifted = keys_wide[:, offset_row:offset_row + height, offset_col:offset_col + width, :]
            shifted = shifted.astype(jnp.float32).reshape(head_shape)
            score_list.append(lax.optimization_barrier(jnp.sum(query_float * shifted, axis=-1)) * factor)
            rows_there = row_places + offset_row - RADIUS
            cols_there = col_places + offset_col - RADIUS
            rows_fine = (rows_there >= 0) & (rows_there < total_rows)
            cols_fine = (cols_there >= 0) & (cols_there < total_cols)
            valid_list.append(rows_fine[:, None] & cols_fine[None, :])
    scores = jnp.stack(score_list, 0)
    valid = jnp.stack(valid_list, 0)[:, None, :, :, None]
    scores = jnp.where(valid, scores, very_negative)
    highest = lax.optimization_barrier(jnp.max(scores, axis=0))
    weights = jnp.exp(scores - highest)
    weights = weights / lax.optimization_barrier(jnp.sum(weights, axis=0))
    total = jnp.zeros(head_shape, jnp.float32)
    index = 0
    for offset_row in range(span):
        for offset_col in range(span):
            shifted = values_wide[:, offset_row:offset_row + height, offset_col:offset_col + width, :]
            shifted = shifted.astype(jnp.float32).reshape(head_shape)
            total = total + weights[index][..., None] * shifted
            index = index + 1
    return total.reshape(queries.shape).astype(jnp.bfloat16)

def reference(view_maps, gain_spatial, spatial_query, spatial_key, spatial_value, spatial_output, gain_temporal, temporal_query, temporal_key, temporal_value, temporal_output):
    normed = rms_norm(view_maps, gain_spatial)
    queries = project(normed, spatial_query).astype(jnp.bfloat16)
    keys = project(normed, spatial_key).astype(jnp.bfloat16)
    values = project(normed, spatial_value).astype(jnp.bfloat16)
    padding = ((0, 0), (RADIUS, RADIUS), (RADIUS, RADIUS), (0, 0))
    keys_wide = jnp.pad(keys, padding)
    values_wide = jnp.pad(values, padding)
    row_places = jnp.arange(MAP_H, dtype=jnp.int32)
    col_places = jnp.arange(MAP_W, dtype=jnp.int32)

    def per_view(items):
        return neighbour(items[0][None], items[1][None], items[2][None], row_places, col_places, MAP_H, MAP_W)[0]
    attended = lax.map(per_view, (queries, keys_wide, values_wide))
    middle = (view_maps.astype(jnp.float32) + project(attended, spatial_output)).astype(jnp.bfloat16)
    normed_time = rms_norm(middle, gain_temporal)
    query_time = project(normed_time, temporal_query).astype(jnp.bfloat16)
    key_time = project(normed_time, temporal_key).astype(jnp.bfloat16)
    value_time = project(normed_time, temporal_value).astype(jnp.bfloat16)
    factor = HEAD_DIM ** (-0.5)

    def per_row(items):
        shape_heads = items[0].shape[:-1] + (HEADS, HEAD_DIM)
        query_float = items[0].astype(jnp.float32).reshape(shape_heads)
        key_float = items[1].astype(jnp.float32).reshape(shape_heads)
        value_float = items[2].astype(jnp.float32).reshape(shape_heads)
        scores = jnp.einsum('qthe,kthe->qkth', query_float, key_float) * factor
        highest = lax.optimization_barrier(jnp.max(scores, axis=1, keepdims=True))
        weights = jnp.exp(scores - highest)
        weights = weights / lax.optimization_barrier(jnp.sum(weights, axis=1, keepdims=True))
        mixed = jnp.einsum('qkth,kthe->qthe', weights, value_float)
        return mixed.reshape(items[0].shape).astype(jnp.bfloat16)
    moved = lax.map(per_row, (jnp.swapaxes(query_time, 0, 1), jnp.swapaxes(key_time, 0, 1), jnp.swapaxes(value_time, 0, 1)))
    attended_time = jnp.swapaxes(moved, 0, 1)
    refined = (middle.astype(jnp.float32) + project(attended_time, temporal_output)).astype(jnp.bfloat16)
    return refined
```

```python
import functools

import jax
import jax.numpy as jnp
from jax import lax
from jax.experimental import pallas as pl
from jax.experimental.pallas import tpu as pltpu
from jax.sharding import PartitionSpec as P

HEAD_DIM = 64
RADIUS = 3
LANES = 256
GROUP = LANES // HEAD_DIM
ROWS = 16
COLS = 8

epsilon = 1e-06
very_negative = -1e30
DIRECTIONS = [(dz, dx) for dz in (-1, 0, 1) for dx in (-1, 0, 1) if dz or dx]


def rms_norm(tokens, gain):
    values = tokens.astype(jnp.float32)
    mean = jnp.mean(values * values, axis=-1, keepdims=True)
    return (values * lax.rsqrt(mean + epsilon) * gain).astype(jnp.bfloat16)


def dot(a, b):
    return jnp.dot(a, b, preferred_element_type=jnp.float32)


def dot_t(a, b):
    return lax.dot_general(a, b, (((1,), (1,)), ((), ())), preferred_element_type=jnp.float32)


def head_masks(rows):
    lane = lax.broadcasted_iota(jnp.int32, (rows, LANES), 1)
    return [(lane >= h * HEAD_DIM) & (lane < (h + 1) * HEAD_DIM) for h in range(GROUP)]


def attend(query, key, value, bias, masks):
    rows = query.shape[0]
    zero = jnp.zeros_like(query)
    stacked = jnp.concatenate([jnp.where(m, query, zero) for m in masks], axis=0)
    scores = dot_t(stacked, key)
    scores = (scores.reshape(GROUP, rows, -1) + bias[None]).reshape(GROUP * rows, -1)
    highest = jnp.max(scores, axis=-1, keepdims=True)
    weights = jnp.exp(scores - highest)
    total = jnp.sum(weights, axis=-1, keepdims=True)
    mixed = dot(weights.astype(jnp.bfloat16), value) * (1.0 / total)
    result = mixed[:rows]
    for h in range(1, GROUP):
        result = jnp.where(masks[h], mixed[h * rows : (h + 1) * rows], result)
    return result


def kernel(
    height, width, side_rows, sizes, x_hbm, gain_s, gain_t, *refs
):
    nv, nz, nx = sizes
    weights_hbm, refs = refs[:8], refs[8:]
    out_ref, wide, sides, w, qbuf, mid, held, normed, kbuf, vbuf, back = refs[:11]
    x_sem, w_sem, hs, hr, ms, mr, bs, br = refs[11:]
    views, own, depth = x_hbm.shape
    share = own // nv
    halo = RADIUS * width
    main = own + 2 * halo
    me, z, x = lax.axis_index("view"), lax.axis_index("row"), lax.axis_index("col")

    x_copy = pltpu.make_async_copy(x_hbm, wide.at[:, pl.ds(halo, own)], x_sem)
    x_copy.start()
    w_copies = [
        pltpu.make_async_copy(weights_hbm[i], w.at[i], w_sem.at[i]) for i in range(8)
    ]
    for copy in w_copies:
        copy.start()

    def there(dz, dx):
        ok = None
        for place, step, count in ((z, dz, nz), (x, dx, nx)):
            if step:
                one = place > 0 if step < 0 else place < count - 1
                ok = one if ok is None else ok & one
        return ok

    def peer(j):
        if nv % 2:
            return lax.rem(me + 1 + j, nv)
        chip, core = me // 2, lax.rem(me, 2)
        k, flip = j // 2 + 1, j % 2
        if j < nv - 2:
            return lax.rem(chip + k, nv // 2) * 2 + (core if flip == 0 else 1 - core)
        return chip * 2 + 1 - core if j == nv - 2 else me

    wide[:, :halo] = jnp.zeros((views, halo, depth), wide.dtype)
    wide[:, halo + own :] = jnp.zeros((views, wide.shape[1] - halo - own, depth), wide.dtype)

    barrier = pltpu.get_barrier_semaphore()
    expected = jnp.int32(nv - 1)
    for dz, dx in DIRECTIONS:
        ok = there(dz, dx)
        expected = expected + ok.astype(jnp.int32)

        @pl.when(ok)
        def _():
            pl.semaphore_signal(
                barrier, inc=1, device_id={"row": z + dz, "col": x + dx},
                device_id_type=pl.DeviceIdType.MESH,
            )

    for j in range(nv - 1):
        pl.semaphore_signal(
            barrier, inc=1, device_id={"view": peer(j)}, device_id_type=pl.DeviceIdType.MESH
        )

    x_copy.wait()
    row = lax.broadcasted_iota(jnp.int32, (2 * side_rows, own), 0)
    cell = lax.broadcasted_iota(jnp.int32, (2 * side_rows, own), 1)
    right = row >= side_rows
    t = jnp.where(right, row - side_rows, row)
    wanted = (t // RADIUS) * width + lax.rem(t, RADIUS) + jnp.where(right, width - RADIUS, 0)
    pick = ((cell == wanted) & (t < RADIUS * height)).astype(jnp.bfloat16)
    for v in range(views):
        packed = dot(pick, wide[v, pl.ds(halo, own)]).astype(jnp.bfloat16)
        sides[v] = packed.reshape(2, side_rows, depth)

    pl.semaphore_wait(barrier, expected)

    def halo_copy(k, v):
        dz, dx = DIRECTIONS[k]
        if dx == 0:
            start = own - halo if dz > 0 else 0
            source = x_hbm.at[v, pl.ds(start, halo)]
            target = wide.at[v, pl.ds(0 if dz > 0 else halo + own, halo)]
        else:
            source = sides.at[v, 0 if dx < 0 else 1]
            block = (0 if dx > 0 else 3) + 1 - dz
            target = wide.at[v, pl.ds(main + block * side_rows, side_rows)]
        return pltpu.make_async_remote_copy(
            src_ref=source, dst_ref=target, send_sem=hs.at[k, v], recv_sem=hr.at[k, v],
            device_id={"row": z + dz, "col": x + dx}, device_id_type=pl.DeviceIdType.MESH,
        )

    for v in range(views):
        for k, (dz, dx) in enumerate(DIRECTIONS):

            @pl.when(there(dz, dx))
            def _():
                halo_copy(k, v).start()

    shape = (own, wide.shape[1])
    query = lax.broadcasted_iota(jnp.int32, shape, 0)
    key = lax.broadcasted_iota(jnp.int32, shape, 1)
    query_row, query_col = query // width, lax.rem(query, width)
    at_side = key >= main
    side_key = key - main
    block, t = side_key // side_rows, lax.rem(side_key, side_rows)
    vertical, on_right = lax.rem(block, 3), block // 3
    key_row = jnp.where(at_side, (vertical - 1) * height + t // RADIUS, key // width - RADIUS)
    key_col = jnp.where(
        at_side, jnp.where(on_right > 0, width, -RADIUS) + lax.rem(t, RADIUS), lax.rem(key, width)
    )
    map_row, map_col = z * height + key_row, x * width + key_col
    seen = (
        (jnp.abs(key_row - query_row) <= RADIUS)
        & (jnp.abs(key_col - query_col) <= RADIUS)
        & (map_row >= 0) & (map_row < nz * height)
        & (map_col >= 0) & (map_col < nx * width)
        & (jnp.logical_not(at_side) | (t < RADIUS * height))
    )
    bias = jnp.where(seen, 0.0, very_negative).astype(jnp.float32)
    scale = HEAD_DIM ** -0.5
    gain = gain_s[...]
    groups = depth // LANES

    own_normed = rms_norm(wide[:, pl.ds(halo, own)].reshape(views * own, depth), gain)
    w_copies[0].wait()
    qbuf[...] = (
        (dot(own_normed, w[0]).astype(jnp.bfloat16) * scale)
        .astype(jnp.bfloat16).reshape(views, own, depth)
    )
    for i in (1, 2, 3):
        w_copies[i].wait()

    def mid_copy(v, target, slot):
        return pltpu.make_async_remote_copy(
            src_ref=mid.at[v, target], dst_ref=held.at[slot, v],
            send_sem=ms.at[target, v], recv_sem=mr.at[slot, v],
            device_id={"view": target}, device_id_type=pl.DeviceIdType.MESH,
        )

    masks = head_masks(own)

    def one_view(v, carry):
        for k, (dz, dx) in enumerate(DIRECTIONS):

            @pl.when(there(-dz, -dx))
            def _():
                halo_copy(k, v).wait_recv()

        tokens = rms_norm(wide[v], gain)
        keys = dot(tokens, w[1]).astype(jnp.bfloat16)
        values = dot(tokens, w[2]).astype(jnp.bfloat16)
        queries = qbuf[v]
        parts = []
        for g in range(groups):
            lanes = slice(g * LANES, (g + 1) * LANES)
            parts.append(
                attend(queries[:, lanes], keys[:, lanes], values[:, lanes], bias, masks)
                .astype(jnp.bfloat16)
            )
        attended = jnp.concatenate(parts, axis=1)
        added = wide[v, pl.ds(halo, own)].astype(jnp.float32) + dot(attended, w[3])
        mid[v] = added.astype(jnp.bfloat16).reshape(nv, share, depth)
        for j in range(nv - 1):
            mid_copy(v, peer(j), me).start()
        held[me, v] = mid[v, me]
        return carry

    lax.fori_loop(0, views, one_view, 0)

    for j in range(nv - 1):
        for v in range(views):
            mid_copy(v, peer(j), peer(j)).wait_recv()
    tokens = rms_norm(held[...].reshape(nv * views * share, depth), gain_t[...])
    normed[...] = tokens.reshape(nv, views * share, depth)
    for i in range(4, 8):
        w_copies[i].wait()
    all_views = nv * views
    cuts = share // COLS

    def cut(array, h):
        part = array.reshape(-1, share, array.shape[-1])[:, h * COLS : (h + 1) * COLS]
        return part.reshape(-1, array.shape[-1])

    keys = dot(tokens, w[5])
    values = dot(tokens, w[6])
    for h in range(cuts):
        kbuf[h] = cut(keys, h).astype(jnp.bfloat16)
        vbuf[h] = cut(values, h).astype(jnp.bfloat16)

    def back_copy(target, slot):
        return pltpu.make_async_remote_copy(
            src_ref=back.at[target], dst_ref=out_ref.at[:, slot],
            send_sem=bs.at[target], recv_sem=br.at[slot],
            device_id={"view": target}, device_id_type=pl.DeviceIdType.MESH,
        )

    step = 1 if nv % 2 else 2
    shape = (step * views * COLS, all_views * COLS)
    query = lax.broadcasted_iota(jnp.int32, shape, 0)
    key = lax.broadcasted_iota(jnp.int32, shape, 1)
    same = jnp.where(lax.rem(query, COLS) == lax.rem(key, COLS), 0.0, very_negative)
    same = same.astype(jnp.float32)
    masks = head_masks(shape[0])
    for first in range(0, nv, step):
        targets = [peer(j) for j in range(first, first + step)]
        chunk = jnp.concatenate([normed[p] for p in targets], axis=0)
        queries = dot(chunk, w[4]).astype(jnp.bfloat16).astype(jnp.float32) * scale
        cut_parts = []
        for h in range(cuts):
            query_cut = cut(queries, h).astype(jnp.bfloat16)
            parts = []
            for g in range(groups):
                lanes = slice(g * LANES, (g + 1) * LANES)
                parts.append(
                    attend(query_cut[:, lanes], kbuf[h, :, lanes], vbuf[h, :, lanes], same, masks)
                )
            cut_parts.append(jnp.concatenate(parts, axis=1).reshape(-1, COLS, depth))
        attended = jnp.concatenate(cut_parts, axis=1).reshape(-1, depth).astype(jnp.bfloat16)
        product = dot(attended, w[7])
        for i, p in enumerate(targets):
            rows = slice(i * views * share, (i + 1) * views * share)
            refined = held[p].reshape(views * share, depth).astype(jnp.float32) + product[rows]
            refined = refined.astype(jnp.bfloat16).reshape(views, share, depth)
            if first + i == nv - 1:
                out_ref[:, p] = refined
            else:
                back[p] = refined
                back_copy(p, me).start()

    for j in range(nv - 1):
        back_copy(peer(j), peer(j)).wait_recv()
    for j in range(nv - 1):
        back_copy(peer(j), me).wait_send()
        for v in range(views):
            mid_copy(v, peer(j), me).wait_send()
    for v in range(views):
        for k, (dz, dx) in enumerate(DIRECTIONS):

            @pl.when(there(dz, dx))
            def _():
                halo_copy(k, v).wait_send()


def body(sizes, view_maps, gain_spatial, *rest):
    spatial, gain_temporal, temporal = rest[:4], rest[4], rest[5:]
    views, height, width, depth = view_maps.shape
    nv = sizes[0]
    own = height * width
    share = own // nv
    side_rows = -(-RADIUS * height // ROWS) * ROWS
    wide = own + 2 * RADIUS * width + 6 * side_rows
    assert own % nv == 0 and share % ROWS == 0 and width % ROWS == 0
    assert height >= RADIUS and width >= RADIUS and depth % LANES == 0
    half = jnp.bfloat16
    hbm = pl.BlockSpec(memory_space=pl.ANY)
    vmem = pl.BlockSpec(memory_space=pltpu.VMEM)
    dma = pltpu.SemaphoreType.DMA
    tokens = nv * views * share
    products = 2 * depth * depth * (8 * views * own + 2 * views * (wide - own))
    result = pl.pallas_call(
        functools.partial(kernel, height, width, side_rows, sizes),
        out_shape=jax.ShapeDtypeStruct((views, nv, share, depth), half),
        in_specs=[hbm, vmem, vmem] + [hbm] * 8,
        out_specs=vmem,
        scratch_shapes=[
            pltpu.VMEM((views, wide, depth), half),
            pltpu.VMEM((views, 2, side_rows, depth), half),
            pltpu.VMEM((8, depth, depth), half),
            pltpu.VMEM((views, own, depth), half),
            pltpu.VMEM((views, nv, share, depth), half),
            pltpu.VMEM((nv, views, share, depth), half),
            pltpu.VMEM((nv, views * share, depth), half),
            pltpu.VMEM((share // COLS, tokens // (share // COLS), depth), half),
            pltpu.VMEM((share // COLS, tokens // (share // COLS), depth), half),
            pltpu.VMEM((nv, views, share, depth), half),
            dma(()),
            dma((8,)),
            dma((len(DIRECTIONS), views)),
            dma((len(DIRECTIONS), views)),
            dma((nv, views)),
            dma((nv, views)),
            dma((nv,)),
            dma((nv,)),
        ],
        compiler_params=pltpu.CompilerParams(
            collective_id=0, has_side_effects=True, vmem_limit_bytes=48 * 1024 * 1024
        ),
        cost_estimate=pl.CostEstimate(
            flops=products, bytes_accessed=16 * depth * depth, transcendentals=0
        ),
    )(
        view_maps.reshape(views, own, depth),
        gain_spatial.reshape(1, depth),
        gain_temporal.reshape(1, depth),
        *spatial,
        *temporal,
    )
    return result.reshape(view_maps.shape)


def solution(mesh):
    sizes = (mesh.shape["view"], mesh.shape["row"], mesh.shape["col"])
    maps = P("view", "row", "col", None)
    return jax.shard_map(
        functools.partial(body, sizes),
        mesh=mesh,
        in_specs=(maps,) + (P(),) * 10,
        out_specs=maps,
        check_vma=False,
    )
```

```python
import functools

import jax
import jax.numpy as jnp
from jax import lax
from jax.experimental import pallas as pl
from jax.experimental.pallas import tpu as pltpu
from jax.sharding import PartitionSpec as P

HEAD_DIM = 64
RADIUS = 3
LANES = 256
GROUP = LANES // HEAD_DIM
ROWS = 16
COLS = 8

epsilon = 1e-06
very_negative = -1e30
DIRECTIONS = [(dz, dx) for dz in (-1, 0, 1) for dx in (-1, 0, 1) if dz or dx]


def rms_norm(tokens, gain):
    values = tokens.astype(jnp.float32)
    mean = jnp.mean(values * values, axis=-1, keepdims=True)
    return (values * lax.rsqrt(mean + epsilon) * gain).astype(jnp.bfloat16)


def dot(a, b):
    return jnp.dot(a, b, preferred_element_type=jnp.float32)


def dot_t(a, b):
    return lax.dot_general(a, b, (((1,), (1,)), ((), ())), preferred_element_type=jnp.float32)


def head_masks(rows):
    lane = lax.broadcasted_iota(jnp.int32, (rows, LANES), 1)
    return [(lane >= h * HEAD_DIM) & (lane < (h + 1) * HEAD_DIM) for h in range(GROUP)]


def attend(query, key, value, bias, masks):
    rows = query.shape[0]
    zero = jnp.zeros_like(query)
    stacked = jnp.concatenate([jnp.where(m, query, zero) for m in masks], axis=0)
    scores = dot_t(stacked, key)
    scores = (scores.reshape(GROUP, rows, -1) + bias[None]).reshape(GROUP * rows, -1)
    highest = jnp.max(scores, axis=-1, keepdims=True)
    weights = jnp.exp(scores - highest)
    total = jnp.sum(weights, axis=-1, keepdims=True)
    mixed = dot(weights.astype(jnp.bfloat16), value) * (1.0 / total)
    result = mixed[:rows]
    for h in range(1, GROUP):
        result = jnp.where(masks[h], mixed[h * rows : (h + 1) * rows], result)
    return result


def kernel(
    height, width, side_rows, sizes, x_hbm, gain_s, gain_t, *refs
):
    nv, nz, nx = sizes
    weights_hbm, refs = refs[:8], refs[8:]
    out_ref, wide, sides, w, qbuf, mid, held, normed, kbuf, vbuf, back, kwide, vwide = refs[:13]
    x_sem, w_sem, hs, hr, ms, mr, bs, br = refs[13:]
    views, own, depth = x_hbm.shape
    share = own // nv
    halo = RADIUS * width
    main = own + 2 * halo
    me, z, x = lax.axis_index("view"), lax.axis_index("row"), lax.axis_index("col")

    x_copy = pltpu.make_async_copy(x_hbm, wide.at[:, pl.ds(halo, own)], x_sem)
    x_copy.start()
    w_copies = [
        pltpu.make_async_copy(weights_hbm[i], w.at[i], w_sem.at[i]) for i in range(8)
    ]
    for copy in w_copies[:4]:
        copy.start()

    def there(dz, dx):
        ok = None
        for place, step, count in ((z, dz, nz), (x, dx, nx)):
            if step:
                one = place > 0 if step < 0 else place < count - 1
                ok = one if ok is None else ok & one
        return ok

    def peer(j):
        if nv % 2:
            return lax.rem(me + 1 + j, nv)
        chip, core = me // 2, lax.rem(me, 2)
        k, flip = j // 2 + 1, j % 2
        if j < nv - 2:
            return lax.rem(chip + k, nv // 2) * 2 + (core if flip == 0 else 1 - core)
        return chip * 2 + 1 - core if j == nv - 2 else me

    wide[:, :halo] = jnp.zeros((views, halo, depth), wide.dtype)
    wide[:, halo + own :] = jnp.zeros((views, wide.shape[1] - halo - own, depth), wide.dtype)

    barrier = pltpu.get_barrier_semaphore()
    expected = jnp.int32(nv - 1)
    for dz, dx in DIRECTIONS:
        ok = there(dz, dx)
        expected = expected + ok.astype(jnp.int32)

        @pl.when(ok)
        def _():
            pl.semaphore_signal(
                barrier, inc=1, device_id={"row": z + dz, "col": x + dx},
                device_id_type=pl.DeviceIdType.MESH,
            )

    for j in range(nv - 1):
        pl.semaphore_signal(
            barrier, inc=1, device_id={"view": peer(j)}, device_id_type=pl.DeviceIdType.MESH
        )

    x_copy.wait()
    row = lax.broadcasted_iota(jnp.int32, (2 * side_rows, own), 0)
    cell = lax.broadcasted_iota(jnp.int32, (2 * side_rows, own), 1)
    right = row >= side_rows
    t = jnp.where(right, row - side_rows, row)
    wanted = (t // RADIUS) * width + lax.rem(t, RADIUS) + jnp.where(right, width - RADIUS, 0)
    pick = ((cell == wanted) & (t < RADIUS * height)).astype(jnp.bfloat16)
    for v in range(views):
        packed = dot(pick, wide[v, pl.ds(halo, own)]).astype(jnp.bfloat16)
        sides[v] = packed.reshape(2, side_rows, depth)

    pl.semaphore_wait(barrier, expected)

    def halo_copy(k, v):
        dz, dx = DIRECTIONS[k]
        if dx == 0:
            start = own - halo if dz > 0 else 0
            source = x_hbm.at[v, pl.ds(start, halo)]
            target = wide.at[v, pl.ds(0 if dz > 0 else halo + own, halo)]
        else:
            source = sides.at[v, 0 if dx < 0 else 1]
            block = (0 if dx > 0 else 3) + 1 - dz
            target = wide.at[v, pl.ds(main + block * side_rows, side_rows)]
        return pltpu.make_async_remote_copy(
            src_ref=source, dst_ref=target, send_sem=hs.at[k, v], recv_sem=hr.at[k, v],
            device_id={"row": z + dz, "col": x + dx}, device_id_type=pl.DeviceIdType.MESH,
        )

    for v in range(views):
        for k, (dz, dx) in enumerate(DIRECTIONS):

            @pl.when(there(dz, dx))
            def _():
                halo_copy(k, v).start()

    shape = (own, wide.shape[1])
    query = lax.broadcasted_iota(jnp.int32, shape, 0)
    key = lax.broadcasted_iota(jnp.int32, shape, 1)
    query_row, query_col = query // width, lax.rem(query, width)
    at_side = key >= main
    side_key = key - main
    block, t = side_key // side_rows, lax.rem(side_key, side_rows)
    vertical, on_right = lax.rem(block, 3), block // 3
    key_row = jnp.where(at_side, (vertical - 1) * height + t // RADIUS, key // width - RADIUS)
    key_col = jnp.where(
        at_side, jnp.where(on_right > 0, width, -RADIUS) + lax.rem(t, RADIUS), lax.rem(key, width)
    )
    map_row, map_col = z * height + key_row, x * width + key_col
    seen = (
        (jnp.abs(key_row - query_row) <= RADIUS)
        & (jnp.abs(key_col - query_col) <= RADIUS)
        & (map_row >= 0) & (map_row < nz * height)
        & (map_col >= 0) & (map_col < nx * width)
        & (jnp.logical_not(at_side) | (t < RADIUS * height))
    )
    bias = jnp.where(seen, 0.0, very_negative).astype(jnp.float32)
    scale = HEAD_DIM ** -0.5
    gain = gain_s[...].reshape(1, depth)
    groups = depth // LANES

    own_normed = rms_norm(wide[:, pl.ds(halo, own)].reshape(views * own, depth), gain)
    w_copies[0].wait()
    qbuf[...] = (
        (dot(own_normed, w[0]).astype(jnp.bfloat16) * scale)
        .astype(jnp.bfloat16).reshape(views, own, depth)
    )
    for copy in w_copies[4:]:
        copy.start()
    for i, wide_buf in ((1, kwide), (2, vwide)):
        w_copies[i].wait()
        wide_buf[:, pl.ds(halo, own)] = (
            dot(own_normed, w[i]).astype(jnp.bfloat16).reshape(views, own, depth)
        )
    w_copies[3].wait()

    def mid_copy(v, target, slot):
        return pltpu.make_async_remote_copy(
            src_ref=mid.at[v, target], dst_ref=held.at[slot, v],
            send_sem=ms.at[target, v], recv_sem=mr.at[slot, v],
            device_id={"view": target}, device_id_type=pl.DeviceIdType.MESH,
        )

    masks = head_masks(own)

    def one_view(v, carry):
        for k, (dz, dx) in enumerate(DIRECTIONS):

            @pl.when(there(-dz, -dx))
            def _():
                halo_copy(k, v).wait_recv()

        around = jnp.concatenate([wide[v, :halo], wide[v, halo + own :]], axis=0)
        tokens = rms_norm(around, gain)
        for i, wide_buf in ((1, kwide), (2, vwide)):
            product = dot(tokens, w[i]).astype(jnp.bfloat16)
            wide_buf[v, :halo] = product[:halo]
            wide_buf[v, halo + own :] = product[halo:]
        keys, values = kwide[v], vwide[v]
        queries = qbuf[v]
        parts = []
        for g in range(groups):
            lanes = slice(g * LANES, (g + 1) * LANES)
            parts.append(
                attend(queries[:, lanes], keys[:, lanes], values[:, lanes], bias, masks)
                .astype(jnp.bfloat16)
            )
        attended = jnp.concatenate(parts, axis=1)
        added = wide[v, pl.ds(halo, own)].astype(jnp.float32) + dot(attended, w[3])
        mid[v] = added.astype(jnp.bfloat16).reshape(nv, share, depth)
        for j in range(nv - 1):
            mid_copy(v, peer(j), me).start()
        held[me, v] = mid[v, me]
        return carry

    lax.fori_loop(0, views, one_view, 0)

    for j in range(nv - 1):
        for v in range(views):
            mid_copy(v, peer(j), peer(j)).wait_recv()
    tokens = rms_norm(held[...].reshape(nv * views * share, depth), gain_t[...].reshape(1, depth))
    normed[...] = tokens.reshape(nv, views * share, depth)
    for i in range(4, 8):
        w_copies[i].wait()
    all_views = nv * views
    cuts = share // COLS

    def cut(array, h):
        part = array.reshape(-1, share, array.shape[-1])[:, h * COLS : (h + 1) * COLS]
        return part.reshape(-1, array.shape[-1])

    keys = dot(tokens, w[5])
    values = dot(tokens, w[6])
    for h in range(cuts):
        kbuf[h] = cut(keys, h).astype(jnp.bfloat16)
        vbuf[h] = cut(values, h).astype(jnp.bfloat16)

    def back_copy(target, slot):
        return pltpu.make_async_remote_copy(
            src_ref=back.at[target], dst_ref=out_ref.at[:, slot],
            send_sem=bs.at[target], recv_sem=br.at[slot],
            device_id={"view": target}, device_id_type=pl.DeviceIdType.MESH,
        )

    step = 1 if nv % 2 else 2
    shape = (step * views * COLS, all_views * COLS)
    query = lax.broadcasted_iota(jnp.int32, shape, 0)
    key = lax.broadcasted_iota(jnp.int32, shape, 1)
    same = jnp.where(lax.rem(query, COLS) == lax.rem(key, COLS), 0.0, very_negative)
    same = same.astype(jnp.float32)
    masks = head_masks(shape[0])
    for first in range(0, nv, step):
        targets = [peer(j) for j in range(first, first + step)]
        chunk = jnp.concatenate([normed[p] for p in targets], axis=0)
        queries = dot(chunk, w[4]).astype(jnp.bfloat16).astype(jnp.float32) * scale
        cut_parts = []
        for h in range(cuts):
            query_cut = cut(queries, h).astype(jnp.bfloat16)
            parts = []
            for g in range(groups):
                lanes = slice(g * LANES, (g + 1) * LANES)
                parts.append(
                    attend(query_cut[:, lanes], kbuf[h, :, lanes], vbuf[h, :, lanes], same, masks)
                )
            cut_parts.append(jnp.concatenate(parts, axis=1).reshape(-1, COLS, depth))
        attended = jnp.concatenate(cut_parts, axis=1).reshape(-1, depth).astype(jnp.bfloat16)
        product = dot(attended, w[7])
        for i, p in enumerate(targets):
            rows = slice(i * views * share, (i + 1) * views * share)
            refined = held[p].reshape(views * share, depth).astype(jnp.float32) + product[rows]
            refined = refined.astype(jnp.bfloat16).reshape(views, share, depth)
            if first + i == nv - 1:
                out_ref[:, p] = refined
            else:
                back[p] = refined
                back_copy(p, me).start()

    for j in range(nv - 1):
        back_copy(peer(j), peer(j)).wait_recv()
    for j in range(nv - 1):
        back_copy(peer(j), me).wait_send()
        for v in range(views):
            mid_copy(v, peer(j), me).wait_send()
    for v in range(views):
        for k, (dz, dx) in enumerate(DIRECTIONS):

            @pl.when(there(dz, dx))
            def _():
                halo_copy(k, v).wait_send()


def body(sizes, view_maps, gain_spatial, *rest):
    spatial, gain_temporal, temporal = rest[:4], rest[4], rest[5:]
    views, height, width, depth = view_maps.shape
    nv = sizes[0]
    own = height * width
    share = own // nv
    side_rows = -(-RADIUS * height // ROWS) * ROWS
    wide = own + 2 * RADIUS * width + 6 * side_rows
    assert own % nv == 0 and share % ROWS == 0 and width % ROWS == 0
    assert height >= RADIUS and width >= RADIUS and depth % LANES == 0
    half = jnp.bfloat16
    hbm = pl.BlockSpec(memory_space=pltpu.HBM)
    vmem = pl.BlockSpec(memory_space=pltpu.VMEM)
    dma = pltpu.SemaphoreType.DMA
    tokens = nv * views * share
    products = 2 * depth * depth * (8 * views * own + 2 * views * (wide - own))
    result = pl.pallas_call(
        functools.partial(kernel, height, width, side_rows, sizes),
        out_shape=jax.ShapeDtypeStruct((views, nv, share, depth), half),
        in_specs=[hbm, vmem, vmem] + [hbm] * 8,
        out_specs=vmem,
        scratch_shapes=[
            pltpu.VMEM((views, wide, depth), half),
            pltpu.VMEM((views, 2, side_rows, depth), half),
            pltpu.VMEM((8, depth, depth), half),
            pltpu.VMEM((views, own, depth), half),
            pltpu.VMEM((views, nv, share, depth), half),
            pltpu.VMEM((nv, views, share, depth), half),
            pltpu.VMEM((nv, views * share, depth), half),
            pltpu.VMEM((share // COLS, tokens // (share // COLS), depth), half),
            pltpu.VMEM((share // COLS, tokens // (share // COLS), depth), half),
            pltpu.VMEM((nv, views, share, depth), half),
            pltpu.VMEM((views, wide, depth), half),
            pltpu.VMEM((views, wide, depth), half),
            dma(()),
            dma((8,)),
            dma((len(DIRECTIONS), views)),
            dma((len(DIRECTIONS), views)),
            dma((nv, views)),
            dma((nv, views)),
            dma((nv,)),
            dma((nv,)),
        ],
        compiler_params=pltpu.CompilerParams(
            collective_id=0, has_side_effects=True, vmem_limit_bytes=56 * 1024 * 1024
        ),
        cost_estimate=pl.CostEstimate(
            flops=products, bytes_accessed=16 * depth * depth, transcendentals=0
        ),
    )(
        view_maps.reshape(views, own, depth),
        gain_spatial,
        gain_temporal,
        *spatial,
        *temporal,
    )
    return result.reshape(view_maps.shape)


def solution(mesh):
    sizes = (mesh.shape["view"], mesh.shape["row"], mesh.shape["col"])
    maps = P("view", "row", "col", None)
    return jax.shard_map(
        functools.partial(body, sizes),
        mesh=mesh,
        in_specs=(maps,) + (P(),) * 10,
        out_specs=maps,
        check_vma=False,
    )
```

```python
import functools

import jax
import jax.numpy as jnp
from jax import lax
from jax.experimental import pallas as pl
from jax.experimental.pallas import tpu as pltpu
from jax.sharding import PartitionSpec as P

HEAD_DIM = 64
RADIUS = 3
LANES = 256
GROUP = LANES // HEAD_DIM
ROWS = 16
COLS = 8

epsilon = 1e-06
very_negative = -1e30
DIRECTIONS = [(dz, dx) for dz in (-1, 0, 1) for dx in (-1, 0, 1) if dz or dx]


def rms_norm(tokens, gain):
    values = tokens.astype(jnp.float32)
    mean = jnp.mean(values * values, axis=-1, keepdims=True)
    return (values * lax.rsqrt(mean + epsilon) * gain).astype(jnp.bfloat16)


def dot(a, b):
    return jnp.dot(a, b, preferred_element_type=jnp.float32)


def dot_t(a, b):
    return lax.dot_general(a, b, (((1,), (1,)), ((), ())), preferred_element_type=jnp.float32)


def head_masks(rows):
    lane = lax.broadcasted_iota(jnp.int32, (rows, LANES), 1)
    return [(lane >= h * HEAD_DIM) & (lane < (h + 1) * HEAD_DIM) for h in range(GROUP)]


def attend(query, key, value, bias, masks):
    rows = query.shape[0]
    zero = jnp.zeros_like(query)
    stacked = jnp.concatenate([jnp.where(m, query, zero) for m in masks], axis=0)
    scores = dot_t(stacked, key)
    scores = (scores.reshape(GROUP, rows, -1) + bias[None]).reshape(GROUP * rows, -1)
    highest = jnp.max(scores, axis=-1, keepdims=True)
    weights = jnp.exp(scores - highest)
    total = jnp.sum(weights, axis=-1, keepdims=True)
    mixed = dot(weights.astype(jnp.bfloat16), value) * (1.0 / total)
    result = mixed[:rows]
    for h in range(1, GROUP):
        result = jnp.where(masks[h], mixed[h * rows : (h + 1) * rows], result)
    return result


def kernel(
    height, width, side_rows, sizes, x_hbm, gain_s, gain_t, *refs
):
    nv, nz, nx = sizes
    weights_hbm, refs = refs[:8], refs[8:]
    out_ref, wide, sides, w, qbuf, mid, held, normed, kbuf, vbuf, qcut, back, kwide, vwide = refs[:14]
    x_sem, w_sem, hs, hr, ms, mr, bs, br = refs[14:]
    views, own, depth = x_hbm.shape
    share = own // 2
    cuts = share // COLS
    halo = RADIUS * width
    main = own + 2 * halo
    me, z, x = lax.axis_index("view"), lax.axis_index("row"), lax.axis_index("col")

    x_copy = pltpu.make_async_copy(x_hbm, wide.at[:, pl.ds(halo, own)], x_sem)
    x_copy.start()
    w_copies = [
        pltpu.make_async_copy(weights_hbm[i], w.at[i], w_sem.at[i]) for i in range(8)
    ]
    for copy in w_copies[:4]:
        copy.start()

    def there(dz, dx):
        ok = None
        for place, step, count in ((z, dz, nz), (x, dx, nx)):
            if step:
                one = place > 0 if step < 0 else place < count - 1
                ok = one if ok is None else ok & one
        return ok

    chip, core = me // 2, lax.rem(me, 2)
    beside = chip * 2 + 1 - core

    def peer(j):
        if j == nv - 2:
            return beside
        there = lax.rem(chip + j // 2 + 1, nv // 2)
        return there * 2 + (core if j % 2 == 0 else 1 - core)

    wide[:, :halo] = jnp.zeros((views, halo, depth), wide.dtype)
    wide[:, halo + own :] = jnp.zeros((views, wide.shape[1] - halo - own, depth), wide.dtype)

    barrier = pltpu.get_barrier_semaphore()
    expected = jnp.int32(nv - 1)
    for dz, dx in DIRECTIONS:
        ok = there(dz, dx)
        expected = expected + ok.astype(jnp.int32)

        @pl.when(ok)
        def _():
            pl.semaphore_signal(
                barrier, inc=1, device_id={"row": z + dz, "col": x + dx},
                device_id_type=pl.DeviceIdType.MESH,
            )

    for j in range(nv - 1):
        pl.semaphore_signal(
            barrier, inc=1, device_id={"view": peer(j)}, device_id_type=pl.DeviceIdType.MESH
        )

    x_copy.wait()
    row = lax.broadcasted_iota(jnp.int32, (2 * side_rows, own), 0)
    cell = lax.broadcasted_iota(jnp.int32, (2 * side_rows, own), 1)
    right = row >= side_rows
    t = jnp.where(right, row - side_rows, row)
    wanted = (t // RADIUS) * width + lax.rem(t, RADIUS) + jnp.where(right, width - RADIUS, 0)
    pick = ((cell == wanted) & (t < RADIUS * height)).astype(jnp.bfloat16)
    for v in range(views):
        packed = dot(pick, wide[v, pl.ds(halo, own)]).astype(jnp.bfloat16)
        sides[v] = packed.reshape(2, side_rows, depth)

    pl.semaphore_wait(barrier, expected)

    def halo_copy(k, v):
        dz, dx = DIRECTIONS[k]
        if dx == 0:
            start = own - halo if dz > 0 else 0
            source = x_hbm.at[v, pl.ds(start, halo)]
            target = wide.at[v, pl.ds(0 if dz > 0 else halo + own, halo)]
        else:
            source = sides.at[v, 0 if dx < 0 else 1]
            block = (0 if dx > 0 else 3) + 1 - dz
            target = wide.at[v, pl.ds(main + block * side_rows, side_rows)]
        return pltpu.make_async_remote_copy(
            src_ref=source, dst_ref=target, send_sem=hs.at[k, v], recv_sem=hr.at[k, v],
            device_id={"row": z + dz, "col": x + dx}, device_id_type=pl.DeviceIdType.MESH,
        )

    for v in range(views):
        for k, (dz, dx) in enumerate(DIRECTIONS):

            @pl.when(there(dz, dx))
            def _():
                halo_copy(k, v).start()

    shape = (own, wide.shape[1])
    query = lax.broadcasted_iota(jnp.int32, shape, 0)
    key = lax.broadcasted_iota(jnp.int32, shape, 1)
    query_row, query_col = query // width, lax.rem(query, width)
    at_side = key >= main
    side_key = key - main
    block, t = side_key // side_rows, lax.rem(side_key, side_rows)
    vertical, on_right = lax.rem(block, 3), block // 3
    key_row = jnp.where(at_side, (vertical - 1) * height + t // RADIUS, key // width - RADIUS)
    key_col = jnp.where(
        at_side, jnp.where(on_right > 0, width, -RADIUS) + lax.rem(t, RADIUS), lax.rem(key, width)
    )
    map_row, map_col = z * height + key_row, x * width + key_col
    seen = (
        (jnp.abs(key_row - query_row) <= RADIUS)
        & (jnp.abs(key_col - query_col) <= RADIUS)
        & (map_row >= 0) & (map_row < nz * height)
        & (map_col >= 0) & (map_col < nx * width)
        & (jnp.logical_not(at_side) | (t < RADIUS * height))
    )
    bias = jnp.where(seen, 0.0, very_negative).astype(jnp.float32)
    scale = HEAD_DIM ** -0.5
    gain = gain_s[...].reshape(1, depth)
    groups = depth // LANES

    own_normed = rms_norm(wide[:, pl.ds(halo, own)].reshape(views * own, depth), gain)
    w_copies[0].wait()
    qbuf[...] = (
        (dot(own_normed, w[0]).astype(jnp.bfloat16) * scale)
        .astype(jnp.bfloat16).reshape(views, own, depth)
    )
    for copy in w_copies[4:]:
        copy.start()
    for i, wide_buf in ((1, kwide), (2, vwide)):
        w_copies[i].wait()
        wide_buf[:, pl.ds(halo, own)] = (
            dot(own_normed, w[i]).astype(jnp.bfloat16).reshape(views, own, depth)
        )
    w_copies[3].wait()

    def mid_copy(v, target, slot):
        return pltpu.make_async_remote_copy(
            src_ref=mid.at[v, lax.rem(target, 2)], dst_ref=held.at[slot, v],
            send_sem=ms.at[target, v], recv_sem=mr.at[slot, v],
            device_id={"view": target}, device_id_type=pl.DeviceIdType.MESH,
        )

    masks = head_masks(own)

    def one_view(v):
        for k, (dz, dx) in enumerate(DIRECTIONS):

            @pl.when(there(-dz, -dx))
            def _():
                halo_copy(k, v).wait_recv()

        around = jnp.concatenate([wide[v, :halo], wide[v, halo + own :]], axis=0)
        tokens = rms_norm(around, gain)
        for i, wide_buf in ((1, kwide), (2, vwide)):
            product = dot(tokens, w[i]).astype(jnp.bfloat16)
            wide_buf[v, :halo] = product[:halo]
            wide_buf[v, halo + own :] = product[halo:]
        keys, values = kwide[v], vwide[v]
        queries = qbuf[v]
        parts = []
        for g in range(groups):
            lanes = slice(g * LANES, (g + 1) * LANES)
            parts.append(
                attend(queries[:, lanes], keys[:, lanes], values[:, lanes], bias, masks)
                .astype(jnp.bfloat16)
            )
        attended = jnp.concatenate(parts, axis=1)
        added = wide[v, pl.ds(halo, own)].astype(jnp.float32) + dot(attended, w[3])
        mid[v] = added.astype(jnp.bfloat16).reshape(2, share, depth)
        for j in range(nv - 1):
            mid_copy(v, peer(j), me).start()
        held[me, v] = mid[v, core]

    gain_time = gain_t[...].reshape(1, depth)

    def cut(array, h):
        part = array.reshape(-1, share, array.shape[-1])[:, h * COLS : (h + 1) * COLS]
        return part.reshape(-1, array.shape[-1])

    def arrived_view(v):
        for j in range(nv - 1):
            mid_copy(v, peer(j), peer(j)).wait_recv()
        tokens = rms_norm(held[:, v].reshape(nv * share, depth), gain_time)
        normed[...] = tokens.reshape(nv, share, depth)
        for i, buf in ((5, kbuf), (6, vbuf)):
            product = dot(tokens, w[i])
            for h in range(cuts):
                buf[h, v] = cut(product, h).astype(jnp.bfloat16)
        mine = normed[pl.ds(chip * 2, 2)].reshape(2 * share, depth)
        queries = dot(mine, w[4]).astype(jnp.bfloat16).astype(jnp.float32) * scale
        queries = queries.reshape(2, cuts, COLS, depth)
        for c in range(2):
            for h in range(cuts):
                qcut[c, h, v] = queries[c, h]

    def turn(v, carry):
        @pl.when(v < views)
        def _():
            one_view(v)

        @pl.when(v > 0)
        def _():
            arrived_view(v - 1)

        return carry

    for i in range(4, 8):
        w_copies[i].wait()
    lax.fori_loop(0, views + 1, turn, 0)

    back_copy = pltpu.make_async_remote_copy(
        src_ref=back, dst_ref=out_ref.at[:, core], send_sem=bs, recv_sem=br,
        device_id={"view": beside}, device_id_type=pl.DeviceIdType.MESH,
    )
    shape = (views * COLS, nv * views * COLS)
    query = lax.broadcasted_iota(jnp.int32, shape, 0)
    key = lax.broadcasted_iota(jnp.int32, shape, 1)
    same = jnp.where(lax.rem(query, COLS) == lax.rem(key, COLS), 0.0, very_negative)
    same = same.astype(jnp.float32)
    masks = head_masks(shape[0])
    for source_core in (1 - core, core):
        cut_parts = []
        for h in range(cuts):
            query_cut = qcut[source_core, h].reshape(shape[0], depth).astype(jnp.bfloat16)
            key_cut = kbuf[h].reshape(shape[1], depth)
            value_cut = vbuf[h].reshape(shape[1], depth)
            parts = []
            for g in range(groups):
                lanes = slice(g * LANES, (g + 1) * LANES)
                parts.append(
                    attend(query_cut[:, lanes], key_cut[:, lanes], value_cut[:, lanes], same, masks)
                )
            cut_parts.append(jnp.concatenate(parts, axis=1).reshape(views, COLS, depth))
        attended = jnp.concatenate(cut_parts, axis=1).reshape(views * share, depth)
        product = dot(attended.astype(jnp.bfloat16), w[7])
        middle = held[chip * 2 + source_core].reshape(views * share, depth)
        refined = (middle.astype(jnp.float32) + product).astype(jnp.bfloat16)
        refined = refined.reshape(views, share, depth)
        if source_core is core:
            out_ref[:, core] = refined
        else:
            back[...] = refined
            back_copy.start()

    back_copy.wait()
    for j in range(nv - 1):
        for v in range(views):
            mid_copy(v, peer(j), me).wait_send()
    for v in range(views):
        for k, (dz, dx) in enumerate(DIRECTIONS):

            @pl.when(there(dz, dx))
            def _():
                halo_copy(k, v).wait_send()


def body(sizes, view_maps, gain_spatial, *rest):
    spatial, gain_temporal, temporal = rest[:4], rest[4], rest[5:]
    views, height, width, depth = view_maps.shape
    nv = sizes[0]
    own = height * width
    share = own // 2
    cuts = share // COLS
    side_rows = -(-RADIUS * height // ROWS) * ROWS
    wide = own + 2 * RADIUS * width + 6 * side_rows
    assert nv % 2 == 0 and own % 2 == 0 and share % ROWS == 0 and width % ROWS == 0
    assert height >= RADIUS and width >= RADIUS and depth % LANES == 0
    half = jnp.bfloat16
    hbm = pl.BlockSpec(memory_space=pltpu.HBM)
    vmem = pl.BlockSpec(memory_space=pltpu.VMEM)
    dma = pltpu.SemaphoreType.DMA
    products = 2 * depth * depth * (8 * views * own + 2 * views * (wide - own))
    result = pl.pallas_call(
        functools.partial(kernel, height, width, side_rows, sizes),
        out_shape=jax.ShapeDtypeStruct((views, 2, share, depth), half),
        in_specs=[hbm, vmem, vmem] + [hbm] * 8,
        out_specs=vmem,
        scratch_shapes=[
            pltpu.VMEM((views, wide, depth), half),
            pltpu.VMEM((views, 2, side_rows, depth), half),
            pltpu.VMEM((8, depth, depth), half),
            pltpu.VMEM((views, own, depth), half),
            pltpu.VMEM((views, 2, share, depth), half),
            pltpu.VMEM((nv, views, share, depth), half),
            pltpu.VMEM((nv, share, depth), half),
            pltpu.VMEM((cuts, views, nv * COLS, depth), half),
            pltpu.VMEM((cuts, views, nv * COLS, depth), half),
            pltpu.VMEM((2, cuts, views, COLS, depth), jnp.float32),
            pltpu.VMEM((views, share, depth), half),
            pltpu.VMEM((views, wide, depth), half),
            pltpu.VMEM((views, wide, depth), half),
            dma(()),
            dma((8,)),
            dma((len(DIRECTIONS), views)),
            dma((len(DIRECTIONS), views)),
            dma((nv, views)),
            dma((nv, views)),
            dma(()),
            dma(()),
        ],
        compiler_params=pltpu.CompilerParams(
            collective_id=0, has_side_effects=True, vmem_limit_bytes=107 * 512 * 1024
        ),
        cost_estimate=pl.CostEstimate(
            flops=products, bytes_accessed=16 * depth * depth, transcendentals=0
        ),
    )(
        view_maps.reshape(views, own, depth),
        gain_spatial,
        gain_temporal,
        *spatial,
        *temporal,
    )
    return result.reshape(view_maps.shape)


def solution(mesh):
    sizes = (mesh.shape["view"], mesh.shape["row"], mesh.shape["col"])
    maps = P("view", "row", "col", None)
    return jax.shard_map(
        functools.partial(body, sizes),
        mesh=mesh,
        in_specs=(maps,) + (P(),) * 10,
        out_specs=maps,
        check_vma=False,
    )
```

```python
import functools

import jax
import jax.numpy as jnp
from jax import lax
from jax.experimental import pallas as pl
from jax.experimental.pallas import tpu as pltpu
from jax.sharding import PartitionSpec as P

HEAD_DIM = 64
RADIUS = 3
LANES = 256
GROUP = LANES // HEAD_DIM
ROWS = 16
COLS = 8

epsilon = 1e-06
very_negative = -1e30
DIRECTIONS = [(dz, dx) for dz in (-1, 0, 1) for dx in (-1, 0, 1) if dz or dx]


def rms_norm(tokens, gain):
    values = tokens.astype(jnp.float32)
    mean = jnp.mean(values * values, axis=-1, keepdims=True)
    return (values * lax.rsqrt(mean + epsilon) * gain).astype(jnp.bfloat16)


def dot(a, b):
    return jnp.dot(a, b, preferred_element_type=jnp.float32)


def dot_t(a, b):
    return lax.dot_general(a, b, (((1,), (1,)), ((), ())), preferred_element_type=jnp.float32)


def head_masks(rows):
    lane = lax.broadcasted_iota(jnp.int32, (rows, LANES), 1)
    return [(lane >= h * HEAD_DIM) & (lane < (h + 1) * HEAD_DIM) for h in range(GROUP)]


def attend(query, key, value, bias, masks):
    rows = query.shape[0]
    zero = jnp.zeros_like(query)
    stacked = jnp.concatenate([jnp.where(m, query, zero) for m in masks], axis=0)
    scores = dot_t(stacked, key)
    scores = (scores.reshape(GROUP, rows, -1) + bias[None]).reshape(GROUP * rows, -1)
    highest = jnp.max(scores, axis=-1, keepdims=True)
    weights = jnp.exp(scores - highest)
    total = jnp.sum(weights, axis=-1, keepdims=True)
    mixed = dot(weights.astype(jnp.bfloat16), value) * (1.0 / total)
    result = mixed[:rows]
    for h in range(1, GROUP):
        result = jnp.where(masks[h], mixed[h * rows : (h + 1) * rows], result)
    return result


def kernel(
    height, width, side_rows, sizes, x_hbm, gain_s_hbm, gain_t_hbm, *refs
):
    nv, nz, nx = sizes
    weights_hbm, refs = refs[:8], refs[8:]
    out_ref, wide, sides, w, qbuf, mid, held, normed, kbuf, vbuf, qcut, back, kwide, vwide, gain_s, gain_t = refs[:16]
    x_sem, w_sem, hs, hr, ms, mr, bs, br, g_sem = refs[16:]
    views, own, depth = x_hbm.shape
    share = own // 2
    cuts = share // COLS
    halo = RADIUS * width
    main = own + 2 * halo
    me, z, x = lax.axis_index("view"), lax.axis_index("row"), lax.axis_index("col")

    x_copy = pltpu.make_async_copy(x_hbm, wide.at[:, pl.ds(halo, own)], x_sem)
    x_copy.start()
    gain_copies = [
        pltpu.make_async_copy(source, target, g_sem.at[i])
        for i, (source, target) in enumerate(((gain_s_hbm, gain_s), (gain_t_hbm, gain_t)))
    ]
    for copy in gain_copies:
        copy.start()
    w_copies = [
        pltpu.make_async_copy(weights_hbm[i], w.at[i], w_sem.at[i]) for i in range(8)
    ]
    for copy in w_copies[:4]:
        copy.start()

    def there(dz, dx):
        ok = None
        for place, step, count in ((z, dz, nz), (x, dx, nx)):
            if step:
                one = place > 0 if step < 0 else place < count - 1
                ok = one if ok is None else ok & one
        return ok

    chip, core = me // 2, lax.rem(me, 2)
    beside = chip * 2 + 1 - core

    def peer(j):
        if j == nv - 2:
            return beside
        there = lax.rem(chip + j // 2 + 1, nv // 2)
        return there * 2 + (core if j % 2 == 0 else 1 - core)

    wide[:, :halo] = jnp.zeros((views, halo, depth), wide.dtype)
    wide[:, halo + own :] = jnp.zeros((views, wide.shape[1] - halo - own, depth), wide.dtype)

    barrier = pltpu.get_barrier_semaphore()
    expected = jnp.int32(nv - 1)
    for dz, dx in DIRECTIONS:
        ok = there(dz, dx)
        expected = expected + ok.astype(jnp.int32)

        @pl.when(ok)
        def _():
            pl.semaphore_signal(
                barrier, inc=1, device_id={"row": z + dz, "col": x + dx},
                device_id_type=pl.DeviceIdType.MESH,
            )

    for j in range(nv - 1):
        pl.semaphore_signal(
            barrier, inc=1, device_id={"view": peer(j)}, device_id_type=pl.DeviceIdType.MESH
        )

    x_copy.wait()
    row = lax.broadcasted_iota(jnp.int32, (2 * side_rows, own), 0)
    cell = lax.broadcasted_iota(jnp.int32, (2 * side_rows, own), 1)
    right = row >= side_rows
    t = jnp.where(right, row - side_rows, row)
    wanted = (t // RADIUS) * width + lax.rem(t, RADIUS) + jnp.where(right, width - RADIUS, 0)
    pick = ((cell == wanted) & (t < RADIUS * height)).astype(jnp.bfloat16)
    for v in range(views):
        packed = dot(pick, wide[v, pl.ds(halo, own)]).astype(jnp.bfloat16)
        sides[v] = packed.reshape(2, side_rows, depth)

    pl.semaphore_wait(barrier, expected)

    def halo_copy(k, v):
        dz, dx = DIRECTIONS[k]
        if dx == 0:
            start = own - halo if dz > 0 else 0
            source = x_hbm.at[v, pl.ds(start, halo)]
            target = wide.at[v, pl.ds(0 if dz > 0 else halo + own, halo)]
        else:
            source = sides.at[v, 0 if dx < 0 else 1]
            block = (0 if dx > 0 else 3) + 1 - dz
            target = wide.at[v, pl.ds(main + block * side_rows, side_rows)]
        return pltpu.make_async_remote_copy(
            src_ref=source, dst_ref=target, send_sem=hs.at[k, v], recv_sem=hr.at[k, v],
            device_id={"row": z + dz, "col": x + dx}, device_id_type=pl.DeviceIdType.MESH,
        )

    for v in range(views):
        for k, (dz, dx) in enumerate(DIRECTIONS):

            @pl.when(there(dz, dx))
            def _():
                halo_copy(k, v).start()

    shape = (own, wide.shape[1])
    query = lax.broadcasted_iota(jnp.int32, shape, 0)
    key = lax.broadcasted_iota(jnp.int32, shape, 1)
    query_row, query_col = query // width, lax.rem(query, width)
    at_side = key >= main
    side_key = key - main
    block, t = side_key // side_rows, lax.rem(side_key, side_rows)
    vertical, on_right = lax.rem(block, 3), block // 3
    key_row = jnp.where(at_side, (vertical - 1) * height + t // RADIUS, key // width - RADIUS)
    key_col = jnp.where(
        at_side, jnp.where(on_right > 0, width, -RADIUS) + lax.rem(t, RADIUS), lax.rem(key, width)
    )
    map_row, map_col = z * height + key_row, x * width + key_col
    seen = (
        (jnp.abs(key_row - query_row) <= RADIUS)
        & (jnp.abs(key_col - query_col) <= RADIUS)
        & (map_row >= 0) & (map_row < nz * height)
        & (map_col >= 0) & (map_col < nx * width)
        & (jnp.logical_not(at_side) | (t < RADIUS * height))
    )
    bias = jnp.where(seen, 0.0, very_negative).astype(jnp.float32)
    scale = HEAD_DIM ** -0.5
    for copy in gain_copies:
        copy.wait()
    gain = gain_s[...].reshape(1, depth)
    groups = depth // LANES

    own_normed = rms_norm(wide[:, pl.ds(halo, own)].reshape(views * own, depth), gain)
    w_copies[0].wait()
    qbuf[...] = (
        (dot(own_normed, w[0]).astype(jnp.bfloat16) * scale)
        .astype(jnp.bfloat16).reshape(views, own, depth)
    )
    for copy in w_copies[4:]:
        copy.start()
    for i, wide_buf in ((1, kwide), (2, vwide)):
        w_copies[i].wait()
        wide_buf[:, pl.ds(halo, own)] = (
            dot(own_normed, w[i]).astype(jnp.bfloat16).reshape(views, own, depth)
        )
    w_copies[3].wait()

    def mid_copy(v, target, slot):
        return pltpu.make_async_remote_copy(
            src_ref=mid.at[v, lax.rem(target, 2)], dst_ref=held.at[slot, v],
            send_sem=ms.at[target, v], recv_sem=mr.at[slot, v],
            device_id={"view": target}, device_id_type=pl.DeviceIdType.MESH,
        )

    masks = head_masks(own)

    batch = 2 if views % 2 == 0 else 1

    def spatial(first):
        batch_views = [first + i for i in range(batch)]
        for v in batch_views:
            for k, (dz, dx) in enumerate(DIRECTIONS):

                @pl.when(there(-dz, -dx))
                def _():
                    halo_copy(k, v).wait_recv()

        around = [part for v in batch_views for part in (wide[v, :halo], wide[v, halo + own :])]
        tokens = rms_norm(jnp.concatenate(around, axis=0), gain)
        outer = wide.shape[1] - own
        for i, wide_buf in ((1, kwide), (2, vwide)):
            product = dot(tokens, w[i]).astype(jnp.bfloat16)
            for n, v in enumerate(batch_views):
                wide_buf[v, :halo] = product[n * outer : n * outer + halo]
                wide_buf[v, halo + own :] = product[n * outer + halo : (n + 1) * outer]
        attended = []
        for v in batch_views:
            parts = []
            for g in range(groups):
                lanes = slice(g * LANES, (g + 1) * LANES)
                parts.append(
                    attend(qbuf[v, :, lanes], kwide[v, :, lanes], vwide[v, :, lanes], bias, masks)
                    .astype(jnp.bfloat16)
                )
            attended.append(jnp.concatenate(parts, axis=1))
        product = dot(jnp.concatenate(attended, axis=0), w[3])
        for n, v in enumerate(batch_views):
            added = wide[v, pl.ds(halo, own)].astype(jnp.float32) + product[n * own : (n + 1) * own]
            mid[v] = added.astype(jnp.bfloat16).reshape(2, share, depth)
            for j in range(nv - 1):
                mid_copy(v, peer(j), me).start()
            held[me, v] = mid[v, core]

    gain_time = gain_t[...].reshape(1, depth)

    def cut(array, h):
        part = array.reshape(-1, share, array.shape[-1])[:, h * COLS : (h + 1) * COLS]
        return part.reshape(-1, array.shape[-1])

    def temporal(first):
        batch_views = [first + i for i in range(batch)]
        for v in batch_views:
            for j in range(nv - 1):
                mid_copy(v, peer(j), peer(j)).wait_recv()
        tokens = jnp.concatenate(
            [held[:, v].reshape(nv * share, depth) for v in batch_views], axis=0
        )
        tokens = rms_norm(tokens, gain_time)
        normed[...] = tokens.reshape(batch, nv, share, depth)
        for i, buf in ((5, kbuf), (6, vbuf)):
            product = dot(tokens, w[i])
            for n, v in enumerate(batch_views):
                rows = product[n * nv * share : (n + 1) * nv * share]
                for h in range(cuts):
                    buf[h, v] = cut(rows, h).astype(jnp.bfloat16)
        mine = normed[:, pl.ds(chip * 2, 2)].reshape(batch * 2 * share, depth)
        queries = dot(mine, w[4]).astype(jnp.bfloat16).astype(jnp.float32) * scale
        queries = queries.reshape(batch, 2, cuts, COLS, depth)
        for n, v in enumerate(batch_views):
            for c in range(2):
                for h in range(cuts):
                    qcut[c, h, v] = queries[n, c, h]

    def turn(t, carry):
        @pl.when(t < views // batch)
        def _():
            spatial(t * batch)

        @pl.when(t > 0)
        def _():
            temporal((t - 1) * batch)

        return carry

    for i in range(4, 8):
        w_copies[i].wait()
    lax.fori_loop(0, views // batch + 1, turn, 0)

    back_copy = pltpu.make_async_remote_copy(
        src_ref=back, dst_ref=out_ref.at[:, core], send_sem=bs, recv_sem=br,
        device_id={"view": beside}, device_id_type=pl.DeviceIdType.MESH,
    )
    shape = (views * COLS, nv * views * COLS)
    query = lax.broadcasted_iota(jnp.int32, shape, 0)
    key = lax.broadcasted_iota(jnp.int32, shape, 1)
    same = jnp.where(lax.rem(query, COLS) == lax.rem(key, COLS), 0.0, very_negative)
    same = same.astype(jnp.float32)
    masks = head_masks(shape[0])
    for source_core in (1 - core, core):
        cut_parts = []
        for h in range(cuts):
            query_cut = qcut[source_core, h].reshape(shape[0], depth).astype(jnp.bfloat16)
            key_cut = kbuf[h].reshape(shape[1], depth)
            value_cut = vbuf[h].reshape(shape[1], depth)
            parts = []
            for g in range(groups):
                lanes = slice(g * LANES, (g + 1) * LANES)
                parts.append(
                    attend(query_cut[:, lanes], key_cut[:, lanes], value_cut[:, lanes], same, masks)
                )
            cut_parts.append(jnp.concatenate(parts, axis=1).reshape(views, COLS, depth))
        attended = jnp.concatenate(cut_parts, axis=1).reshape(views * share, depth)
        product = dot(attended.astype(jnp.bfloat16), w[7])
        middle = held[chip * 2 + source_core].reshape(views * share, depth)
        refined = (middle.astype(jnp.float32) + product).astype(jnp.bfloat16)
        refined = refined.reshape(views, share, depth)
        if source_core is core:
            out_ref[:, core] = refined
        else:
            back[...] = refined
            back_copy.start()

    back_copy.wait()
    for j in range(nv - 1):
        for v in range(views):
            mid_copy(v, peer(j), me).wait_send()
    for v in range(views):
        for k, (dz, dx) in enumerate(DIRECTIONS):

            @pl.when(there(dz, dx))
            def _():
                halo_copy(k, v).wait_send()


def body(sizes, view_maps, gain_spatial, *rest):
    spatial, gain_temporal, temporal = rest[:4], rest[4], rest[5:]
    views, height, width, depth = view_maps.shape
    nv = sizes[0]
    own = height * width
    share = own // 2
    cuts = share // COLS
    side_rows = -(-RADIUS * height // ROWS) * ROWS
    wide = own + 2 * RADIUS * width + 6 * side_rows
    assert nv % 2 == 0 and own % 2 == 0 and share % ROWS == 0 and width % ROWS == 0
    assert height >= RADIUS and width >= RADIUS and depth % LANES == 0
    half = jnp.bfloat16
    hbm = pl.BlockSpec(memory_space=pltpu.HBM)
    vmem = pl.BlockSpec(memory_space=pltpu.VMEM)
    dma = pltpu.SemaphoreType.DMA
    products = 2 * depth * depth * (8 * views * own + 2 * views * (wide - own))
    result = pl.pallas_call(
        functools.partial(kernel, height, width, side_rows, sizes),
        out_shape=jax.ShapeDtypeStruct((views, 2, share, depth), half),
        in_specs=[hbm] * 11,
        out_specs=vmem,
        scratch_shapes=[
            pltpu.VMEM((views, wide, depth), half),
            pltpu.VMEM((views, 2, side_rows, depth), half),
            pltpu.VMEM((8, depth, depth), half),
            pltpu.VMEM((views, own, depth), half),
            pltpu.VMEM((views, 2, share, depth), half),
            pltpu.VMEM((nv, views, share, depth), half),
            pltpu.VMEM((2 if views % 2 == 0 else 1, nv, share, depth), half),
            pltpu.VMEM((cuts, views, nv * COLS, depth), half),
            pltpu.VMEM((cuts, views, nv * COLS, depth), half),
            pltpu.VMEM((2, cuts, views, COLS, depth), jnp.float32),
            pltpu.VMEM((views, share, depth), half),
            pltpu.VMEM((views, wide, depth), half),
            pltpu.VMEM((views, wide, depth), half),
            pltpu.VMEM((depth,), jnp.float32),
            pltpu.VMEM((depth,), jnp.float32),
            dma(()),
            dma((8,)),
            dma((len(DIRECTIONS), views)),
            dma((len(DIRECTIONS), views)),
            dma((nv, views)),
            dma((nv, views)),
            dma(()),
            dma(()),
            dma((2,)),
        ],
        compiler_params=pltpu.CompilerParams(
            collective_id=0, has_side_effects=True, vmem_limit_bytes=107 * 512 * 1024
        ),
        cost_estimate=pl.CostEstimate(
            flops=products, bytes_accessed=16 * depth * depth, transcendentals=0
        ),
    )(
        view_maps.reshape(views, own, depth),
        gain_spatial,
        gain_temporal,
        *spatial,
        *temporal,
    )
    return result.reshape(view_maps.shape)


def solution(mesh):
    sizes = (mesh.shape["view"], mesh.shape["row"], mesh.shape["col"])
    maps = P("view", "row", "col", None)
    return jax.shard_map(
        functools.partial(body, sizes),
        mesh=mesh,
        in_specs=(maps,) + (P(),) * 10,
        out_specs=maps,
        check_vma=False,
    )
```

```python
import functools

import jax
import jax.numpy as jnp
from jax import lax
from jax.experimental import pallas as pl
from jax.experimental.pallas import tpu as pltpu
from jax.sharding import PartitionSpec as P

HEAD_DIM = 64
RADIUS = 3
LANES = 256
GROUP = LANES // HEAD_DIM
ROWS = 16
COLS = 8

epsilon = 1e-06
very_negative = -1e30
DIRECTIONS = [(dz, dx) for dz in (-1, 0, 1) for dx in (-1, 0, 1) if dz or dx]


def rms_norm(tokens, gain):
    values = tokens.astype(jnp.float32)
    mean = jnp.mean(values * values, axis=-1, keepdims=True)
    return (values * lax.rsqrt(mean + epsilon) * gain).astype(jnp.bfloat16)


def dot(a, b):
    return jnp.dot(a, b, preferred_element_type=jnp.float32)


def dot_t(a, b):
    return lax.dot_general(a, b, (((1,), (1,)), ((), ())), preferred_element_type=jnp.float32)


def head_masks(rows):
    lane = lax.broadcasted_iota(jnp.int32, (rows, LANES), 1)
    return [(lane >= h * HEAD_DIM) & (lane < (h + 1) * HEAD_DIM) for h in range(GROUP)]


def attend(query, key, value, bias, masks):
    rows = query.shape[0]
    zero = jnp.zeros_like(query)
    stacked = jnp.concatenate([jnp.where(m, query, zero) for m in masks], axis=0)
    scores = dot_t(stacked, key)
    scores = (scores.reshape(GROUP, rows, -1) + bias[None]).reshape(GROUP * rows, -1)
    highest = jnp.max(scores, axis=-1, keepdims=True)
    weights = jnp.exp(scores - highest)
    total = jnp.sum(weights, axis=-1, keepdims=True)
    mixed = dot(weights.astype(jnp.bfloat16), value) * (1.0 / total)
    result = mixed[:rows]
    for h in range(1, GROUP):
        result = jnp.where(masks[h], mixed[h * rows : (h + 1) * rows], result)
    return result


def kernel(
    height, width, side_rows, sizes, x_hbm, gains_hbm, *refs
):
    nv, nz, nx = sizes
    weights_hbm, refs = refs[:8], refs[8:]
    out_ref, wide, sides, w, qbuf, mid, held, normed, kbuf, vbuf, qcut, back, kwide, vwide, gains = refs[:15]
    x_sem, w_sem, hs, hr, ms, mr, bs, br, g_sem = refs[15:]
    views, own, depth = x_hbm.shape
    share = own // 2
    cuts = share // COLS
    halo = RADIUS * width
    main = own + 2 * halo
    me, z, x = lax.axis_index("view"), lax.axis_index("row"), lax.axis_index("col")

    x_copy = pltpu.make_async_copy(x_hbm, wide.at[:, pl.ds(halo, own)], x_sem)
    x_copy.start()
    gain_copy = pltpu.make_async_copy(gains_hbm, gains, g_sem)
    gain_copy.start()
    w_copies = [
        pltpu.make_async_copy(weights_hbm[i], w.at[i], w_sem.at[i]) for i in range(8)
    ]
    for copy in w_copies[:4]:
        copy.start()

    def there(dz, dx):
        ok = None
        for place, step, count in ((z, dz, nz), (x, dx, nx)):
            if step:
                one = place > 0 if step < 0 else place < count - 1
                ok = one if ok is None else ok & one
        return ok

    chip, core = me // 2, lax.rem(me, 2)
    beside = chip * 2 + 1 - core

    def peer(j):
        if j == nv - 2:
            return beside
        there = lax.rem(chip + j // 2 + 1, nv // 2)
        return there * 2 + (core if j % 2 == 0 else 1 - core)

    wide[:, :halo] = jnp.zeros((views, halo, depth), wide.dtype)
    wide[:, halo + own :] = jnp.zeros((views, wide.shape[1] - halo - own, depth), wide.dtype)

    barrier = pltpu.get_barrier_semaphore()
    expected = jnp.int32(nv - 1)
    for dz, dx in DIRECTIONS:
        ok = there(dz, dx)
        expected = expected + ok.astype(jnp.int32)

        @pl.when(ok)
        def _():
            pl.semaphore_signal(
                barrier, inc=1, device_id={"row": z + dz, "col": x + dx},
                device_id_type=pl.DeviceIdType.MESH,
            )

    for j in range(nv - 1):
        pl.semaphore_signal(
            barrier, inc=1, device_id={"view": peer(j)}, device_id_type=pl.DeviceIdType.MESH
        )

    pl.semaphore_wait(barrier, expected)

    def halo_copy(k, v):
        dz, dx = DIRECTIONS[k]
        if dx == 0:
            start = own - halo if dz > 0 else 0
            source = x_hbm.at[v, pl.ds(start, halo)]
            target = wide.at[v, pl.ds(0 if dz > 0 else halo + own, halo)]
        else:
            source = sides.at[v, 0 if dx < 0 else 1]
            block = (0 if dx > 0 else 3) + 1 - dz
            target = wide.at[v, pl.ds(main + block * side_rows, side_rows)]
        return pltpu.make_async_remote_copy(
            src_ref=source, dst_ref=target, send_sem=hs.at[k, v], recv_sem=hr.at[k, v],
            device_id={"row": z + dz, "col": x + dx}, device_id_type=pl.DeviceIdType.MESH,
        )

    def send(v, wanted):
        for k, (dz, dx) in enumerate(DIRECTIONS):
            if wanted(dx):

                @pl.when(there(dz, dx))
                def _():
                    halo_copy(k, v).start()

    batch = 2 if views % 2 == 0 else 1
    for v in range(batch):
        send(v, lambda dx: dx == 0)
    x_copy.wait()
    row = lax.broadcasted_iota(jnp.int32, (2 * side_rows, own), 0)
    cell = lax.broadcasted_iota(jnp.int32, (2 * side_rows, own), 1)
    right = row >= side_rows
    t = jnp.where(right, row - side_rows, row)
    wanted = (t // RADIUS) * width + lax.rem(t, RADIUS) + jnp.where(right, width - RADIUS, 0)
    pick = ((cell == wanted) & (t < RADIUS * height)).astype(jnp.bfloat16)
    for v in range(views):
        packed = dot(pick, wide[v, pl.ds(halo, own)]).astype(jnp.bfloat16)
        sides[v] = packed.reshape(2, side_rows, depth)
        if v >= batch:
            send(v, lambda dx: dx == 0)
        send(v, lambda dx: dx != 0)

    shape = (own, wide.shape[1])
    query = lax.broadcasted_iota(jnp.int32, shape, 0)
    key = lax.broadcasted_iota(jnp.int32, shape, 1)
    query_row, query_col = query // width, lax.rem(query, width)
    at_side = key >= main
    side_key = key - main
    block, t = side_key // side_rows, lax.rem(side_key, side_rows)
    vertical, on_right = lax.rem(block, 3), block // 3
    key_row = jnp.where(at_side, (vertical - 1) * height + t // RADIUS, key // width - RADIUS)
    key_col = jnp.where(
        at_side, jnp.where(on_right > 0, width, -RADIUS) + lax.rem(t, RADIUS), lax.rem(key, width)
    )
    map_row, map_col = z * height + key_row, x * width + key_col
    seen = (
        (jnp.abs(key_row - query_row) <= RADIUS)
        & (jnp.abs(key_col - query_col) <= RADIUS)
        & (map_row >= 0) & (map_row < nz * height)
        & (map_col >= 0) & (map_col < nx * width)
        & (jnp.logical_not(at_side) | (t < RADIUS * height))
    )
    bias = jnp.where(seen, 0.0, very_negative).astype(jnp.float32)
    scale = HEAD_DIM ** -0.5
    gain_copy.wait()
    gain = gains[0:1]
    groups = depth // LANES

    own_normed = rms_norm(wide[:, pl.ds(halo, own)].reshape(views * own, depth), gain)
    w_copies[0].wait()
    qbuf[...] = (
        (dot(own_normed, w[0]).astype(jnp.bfloat16) * scale)
        .astype(jnp.bfloat16).reshape(views, own, depth)
    )
    for copy in w_copies[4:]:
        copy.start()
    for i, wide_buf in ((1, kwide), (2, vwide)):
        w_copies[i].wait()
        wide_buf[:, pl.ds(halo, own)] = (
            dot(own_normed, w[i]).astype(jnp.bfloat16).reshape(views, own, depth)
        )
    w_copies[3].wait()

    def mid_copy(v, target, slot):
        return pltpu.make_async_remote_copy(
            src_ref=mid.at[v, lax.rem(target, 2)], dst_ref=held.at[slot, v],
            send_sem=ms.at[target, v], recv_sem=mr.at[slot, v],
            device_id={"view": target}, device_id_type=pl.DeviceIdType.MESH,
        )

    masks = head_masks(own)

    def spatial(first):
        batch_views = [first + i for i in range(batch)]
        for v in batch_views:
            for k, (dz, dx) in enumerate(DIRECTIONS):

                @pl.when(there(-dz, -dx))
                def _():
                    halo_copy(k, v).wait_recv()

        around = [part for v in batch_views for part in (wide[v, :halo], wide[v, halo + own :])]
        tokens = rms_norm(jnp.concatenate(around, axis=0), gain)
        outer = wide.shape[1] - own
        for i, wide_buf in ((1, kwide), (2, vwide)):
            product = dot(tokens, w[i]).astype(jnp.bfloat16)
            for n, v in enumerate(batch_views):
                wide_buf[v, :halo] = product[n * outer : n * outer + halo]
                wide_buf[v, halo + own :] = product[n * outer + halo : (n + 1) * outer]
        for v in batch_views:
            parts = []
            for g in range(groups):
                lanes = slice(g * LANES, (g + 1) * LANES)
                parts.append(
                    attend(qbuf[v, :, lanes], kwide[v, :, lanes], vwide[v, :, lanes], bias, masks)
                    .astype(jnp.bfloat16)
                )
            product = dot(jnp.concatenate(parts, axis=1), w[3])
            added = wide[v, pl.ds(halo, own)].astype(jnp.float32) + product
            mid[v] = added.astype(jnp.bfloat16).reshape(2, share, depth)
            for j in range(nv - 1):
                mid_copy(v, peer(j), me).start()
            held[me, v] = mid[v, core]

    gain_time = gains[1:2]

    def cut(array, h):
        part = array.reshape(-1, share, array.shape[-1])[:, h * COLS : (h + 1) * COLS]
        return part.reshape(-1, array.shape[-1])

    def temporal(first):
        batch_views = [first + i for i in range(batch)]
        for v in batch_views:
            for j in range(nv - 1):
                mid_copy(v, peer(j), peer(j)).wait_recv()
        tokens = jnp.concatenate(
            [held[:, v].reshape(nv * share, depth) for v in batch_views], axis=0
        )
        tokens = rms_norm(tokens, gain_time)
        normed[...] = tokens.reshape(batch, nv, share, depth)
        for i, buf in ((5, kbuf), (6, vbuf)):
            product = dot(tokens, w[i])
            for n, v in enumerate(batch_views):
                rows = product[n * nv * share : (n + 1) * nv * share]
                for h in range(cuts):
                    buf[h, v] = cut(rows, h).astype(jnp.bfloat16)
        mine = normed[:, pl.ds(chip * 2, 2)].reshape(batch * 2 * share, depth)
        queries = dot(mine, w[4]).astype(jnp.bfloat16).astype(jnp.float32) * scale
        queries = queries.reshape(batch, 2, cuts, COLS, depth)
        for n, v in enumerate(batch_views):
            for c in range(2):
                for h in range(cuts):
                    qcut[c, h, v] = queries[n, c, h]

    def turn(t, carry):
        @pl.when(t < views // batch)
        def _():
            spatial(t * batch)

        @pl.when(t > 0)
        def _():
            temporal((t - 1) * batch)

        return carry

    for i in range(4, 8):
        w_copies[i].wait()
    lax.fori_loop(0, views // batch + 1, turn, 0)

    back_copy = pltpu.make_async_remote_copy(
        src_ref=back, dst_ref=out_ref.at[:, core], send_sem=bs, recv_sem=br,
        device_id={"view": beside}, device_id_type=pl.DeviceIdType.MESH,
    )
    shape = (views * COLS, nv * views * COLS)
    query = lax.broadcasted_iota(jnp.int32, shape, 0)
    key = lax.broadcasted_iota(jnp.int32, shape, 1)
    same = jnp.where(lax.rem(query, COLS) == lax.rem(key, COLS), 0.0, very_negative)
    same = same.astype(jnp.float32)
    masks = head_masks(shape[0])
    for source_core in (1 - core, core):
        cut_parts = []
        for h in range(cuts):
            query_cut = qcut[source_core, h].reshape(shape[0], depth).astype(jnp.bfloat16)
            key_cut = kbuf[h].reshape(shape[1], depth)
            value_cut = vbuf[h].reshape(shape[1], depth)
            parts = []
            for g in range(groups):
                lanes = slice(g * LANES, (g + 1) * LANES)
                parts.append(
                    attend(query_cut[:, lanes], key_cut[:, lanes], value_cut[:, lanes], same, masks)
                )
            cut_parts.append(jnp.concatenate(parts, axis=1).reshape(views, COLS, depth))
        attended = jnp.concatenate(cut_parts, axis=1).reshape(views * share, depth)
        product = dot(attended.astype(jnp.bfloat16), w[7])
        middle = held[chip * 2 + source_core].reshape(views * share, depth)
        refined = (middle.astype(jnp.float32) + product).astype(jnp.bfloat16)
        refined = refined.reshape(views, share, depth)
        if source_core is core:
            out_ref[:, core] = refined
        else:
            back[...] = refined
            back_copy.start()

    back_copy.wait()
    for j in range(nv - 1):
        for v in range(views):
            mid_copy(v, peer(j), me).wait_send()
    for v in range(views):
        for k, (dz, dx) in enumerate(DIRECTIONS):

            @pl.when(there(dz, dx))
            def _():
                halo_copy(k, v).wait_send()


def body(sizes, view_maps, gain_spatial, *rest):
    spatial, gain_temporal, temporal = rest[:4], rest[4], rest[5:]
    views, height, width, depth = view_maps.shape
    nv = sizes[0]
    own = height * width
    share = own // 2
    cuts = share // COLS
    side_rows = -(-RADIUS * height // ROWS) * ROWS
    wide = own + 2 * RADIUS * width + 6 * side_rows
    assert nv % 2 == 0 and own % 2 == 0 and share % ROWS == 0 and width % ROWS == 0
    assert height >= RADIUS and width >= RADIUS and depth % LANES == 0
    half = jnp.bfloat16
    hbm = pl.BlockSpec(memory_space=pltpu.HBM)
    vmem = pl.BlockSpec(memory_space=pltpu.VMEM)
    dma = pltpu.SemaphoreType.DMA
    products = 2 * depth * depth * (8 * views * own + 2 * views * (wide - own))
    result = pl.pallas_call(
        functools.partial(kernel, height, width, side_rows, sizes),
        out_shape=jax.ShapeDtypeStruct((views, 2, share, depth), half),
        in_specs=[hbm] * 10,
        out_specs=vmem,
        scratch_shapes=[
            pltpu.VMEM((views, wide, depth), half),
            pltpu.VMEM((views, 2, side_rows, depth), half),
            pltpu.VMEM((8, depth, depth), half),
            pltpu.VMEM((views, own, depth), half),
            pltpu.VMEM((views, 2, share, depth), half),
            pltpu.VMEM((nv, views, share, depth), half),
            pltpu.VMEM((2 if views % 2 == 0 else 1, nv, share, depth), half),
            pltpu.VMEM((cuts, views, nv * COLS, depth), half),
            pltpu.VMEM((cuts, views, nv * COLS, depth), half),
            pltpu.VMEM((2, cuts, views, COLS, depth), jnp.float32),
            pltpu.VMEM((views, share, depth), half),
            pltpu.VMEM((views, wide, depth), half),
            pltpu.VMEM((views, wide, depth), half),
            pltpu.VMEM((2, depth), jnp.float32),
            dma(()),
            dma((8,)),
            dma((len(DIRECTIONS), views)),
            dma((len(DIRECTIONS), views)),
            dma((nv, views)),
            dma((nv, views)),
            dma(()),
            dma(()),
            dma(()),
        ],
        compiler_params=pltpu.CompilerParams(
            collective_id=0, has_side_effects=True, vmem_limit_bytes=107 * 512 * 1024
        ),
        cost_estimate=pl.CostEstimate(
            flops=products, bytes_accessed=16 * depth * depth, transcendentals=0
        ),
    )(
        view_maps.reshape(views, own, depth),
        jnp.stack([gain_spatial, gain_temporal]),
        *spatial,
        *temporal,
    )
    return result.reshape(view_maps.shape)


def solution(mesh):
    sizes = (mesh.shape["view"], mesh.shape["row"], mesh.shape["col"])
    maps = P("view", "row", "col", None)
    return jax.shard_map(
        functools.partial(body, sizes),
        mesh=mesh,
        in_specs=(maps,) + (P(),) * 10,
        out_specs=maps,
        check_vma=False,
    )
```

```python
import functools

import jax
import jax.numpy as jnp
from jax import lax
from jax.experimental import pallas as pl
from jax.experimental.pallas import tpu as pltpu
from jax.sharding import PartitionSpec as P

HEAD_DIM = 64
RADIUS = 3
LANES = 256
GROUP = LANES // HEAD_DIM
ROWS = 16
COLS = 8

epsilon = 1e-06
very_negative = -1e30
DIRECTIONS = [(dz, dx) for dz in (-1, 0, 1) for dx in (-1, 0, 1) if dz or dx]


def rms_norm(tokens, gain):
    values = tokens.astype(jnp.float32)
    mean = jnp.mean(values * values, axis=-1, keepdims=True)
    return (values * lax.rsqrt(mean + epsilon) * gain).astype(jnp.bfloat16)


def dot(a, b):
    return jnp.dot(a, b, preferred_element_type=jnp.float32)


def dot_t(a, b):
    return lax.dot_general(a, b, (((1,), (1,)), ((), ())), preferred_element_type=jnp.float32)


def head_masks(rows):
    lane = lax.broadcasted_iota(jnp.int32, (rows, LANES), 1)
    return [(lane >= h * HEAD_DIM) & (lane < (h + 1) * HEAD_DIM) for h in range(GROUP)]


def attend(query, key, value, bias, masks):
    rows = query.shape[0]
    zero = jnp.zeros_like(query)
    stacked = jnp.concatenate([jnp.where(m, query, zero) for m in masks], axis=0)
    scores = dot_t(stacked, key)
    scores = (scores.reshape(GROUP, rows, -1) + bias[None]).reshape(GROUP * rows, -1)
    highest = jnp.max(scores, axis=-1, keepdims=True)
    weights = jnp.exp(scores - highest)
    total = jnp.sum(weights, axis=-1, keepdims=True)
    mixed = dot(weights.astype(jnp.bfloat16), value) * (1.0 / total)
    result = mixed[:rows]
    for h in range(1, GROUP):
        result = jnp.where(masks[h], mixed[h * rows : (h + 1) * rows], result)
    return result


def kernel(
    height, width, side_rows, sizes, x_hbm, gains_hbm, *refs
):
    nv, nz, nx = sizes
    weights_hbm, refs = refs[:8], refs[8:]
    out_ref, wide, sides, w, qbuf, mid, held, normed, kbuf, vbuf, qcut, back, kwide, vwide, gains = refs[:15]
    x_sem, w_sem, hs, hr, ms, mr, bs, br, g_sem = refs[15:]
    views, own, depth = x_hbm.shape
    share = own // 2
    cuts = share // COLS
    halo = RADIUS * width
    main = own + 2 * halo
    me, z, x = lax.axis_index("view"), lax.axis_index("row"), lax.axis_index("col")

    x_copy = pltpu.make_async_copy(x_hbm, wide.at[:, pl.ds(halo, own)], x_sem)
    x_copy.start()
    gain_copy = pltpu.make_async_copy(gains_hbm, gains, g_sem)
    gain_copy.start()
    w_copies = [
        pltpu.make_async_copy(weights_hbm[i], w.at[i], w_sem.at[i]) for i in range(8)
    ]
    for copy in w_copies[:4]:
        copy.start()

    def there(dz, dx):
        ok = None
        for place, step, count in ((z, dz, nz), (x, dx, nx)):
            if step:
                one = place > 0 if step < 0 else place < count - 1
                ok = one if ok is None else ok & one
        return ok

    chip, core = me // 2, lax.rem(me, 2)
    beside = chip * 2 + 1 - core

    def peer(j):
        if j == nv - 2:
            return beside
        there = lax.rem(chip + j // 2 + 1, nv // 2)
        return there * 2 + (core if j % 2 == 0 else 1 - core)

    wide[:, :halo] = jnp.zeros((views, halo, depth), wide.dtype)
    wide[:, halo + own :] = jnp.zeros((views, wide.shape[1] - halo - own, depth), wide.dtype)

    barrier = pltpu.get_barrier_semaphore()
    expected = jnp.int32(nv - 1)
    for dz, dx in DIRECTIONS:
        ok = there(dz, dx)
        expected = expected + ok.astype(jnp.int32)

        @pl.when(ok)
        def _():
            pl.semaphore_signal(
                barrier, inc=1, device_id={"row": z + dz, "col": x + dx},
                device_id_type=pl.DeviceIdType.MESH,
            )

    for j in range(nv - 1):
        pl.semaphore_signal(
            barrier, inc=1, device_id={"view": peer(j)}, device_id_type=pl.DeviceIdType.MESH
        )

    pl.semaphore_wait(barrier, expected)

    def halo_copy(k, v):
        dz, dx = DIRECTIONS[k]
        if dx == 0:
            start = own - halo if dz > 0 else 0
            source = x_hbm.at[v, pl.ds(start, halo)]
            target = wide.at[v, pl.ds(0 if dz > 0 else halo + own, halo)]
        else:
            source = sides.at[v, 0 if dx < 0 else 1]
            block = (0 if dx > 0 else 3) + 1 - dz
            target = wide.at[v, pl.ds(main + block * side_rows, side_rows)]
        return pltpu.make_async_remote_copy(
            src_ref=source, dst_ref=target, send_sem=hs.at[k, v], recv_sem=hr.at[k, v],
            device_id={"row": z + dz, "col": x + dx}, device_id_type=pl.DeviceIdType.MESH,
        )

    def send(v, wanted):
        for k, (dz, dx) in enumerate(DIRECTIONS):
            if wanted(dx):

                @pl.when(there(dz, dx))
                def _():
                    halo_copy(k, v).start()

    early = min(2, views)
    for v in range(early):
        send(v, lambda dx: dx == 0)
    x_copy.wait()
    row = lax.broadcasted_iota(jnp.int32, (2 * side_rows, own), 0)
    cell = lax.broadcasted_iota(jnp.int32, (2 * side_rows, own), 1)
    right = row >= side_rows
    t = jnp.where(right, row - side_rows, row)
    wanted = (t // RADIUS) * width + lax.rem(t, RADIUS) + jnp.where(right, width - RADIUS, 0)
    pick = ((cell == wanted) & (t < RADIUS * height)).astype(jnp.bfloat16)
    for v in range(views):
        packed = dot(pick, wide[v, pl.ds(halo, own)]).astype(jnp.bfloat16)
        sides[v] = packed.reshape(2, side_rows, depth)
        if v >= early:
            send(v, lambda dx: dx == 0)
        send(v, lambda dx: dx != 0)

    shape = (own, wide.shape[1])
    query = lax.broadcasted_iota(jnp.int32, shape, 0)
    key = lax.broadcasted_iota(jnp.int32, shape, 1)
    query_row, query_col = query // width, lax.rem(query, width)
    at_side = key >= main
    side_key = key - main
    block, t = side_key // side_rows, lax.rem(side_key, side_rows)
    vertical, on_right = lax.rem(block, 3), block // 3
    key_row = jnp.where(at_side, (vertical - 1) * height + t // RADIUS, key // width - RADIUS)
    key_col = jnp.where(
        at_side, jnp.where(on_right > 0, width, -RADIUS) + lax.rem(t, RADIUS), lax.rem(key, width)
    )
    map_row, map_col = z * height + key_row, x * width + key_col
    seen = (
        (jnp.abs(key_row - query_row) <= RADIUS)
        & (jnp.abs(key_col - query_col) <= RADIUS)
        & (map_row >= 0) & (map_row < nz * height)
        & (map_col >= 0) & (map_col < nx * width)
        & (jnp.logical_not(at_side) | (t < RADIUS * height))
    )
    bias = jnp.where(seen, 0.0, very_negative).astype(jnp.float32)
    scale = HEAD_DIM ** -0.5
    gain_copy.wait()
    gain_rows = gains[...].reshape(1, 2 * depth)
    gain = gain_rows[:, :depth]
    groups = depth // LANES

    own_normed = rms_norm(wide[:, pl.ds(halo, own)].reshape(views * own, depth), gain)
    w_copies[0].wait()
    qbuf[...] = (
        (dot(own_normed, w[0]).astype(jnp.bfloat16) * scale)
        .astype(jnp.bfloat16).reshape(views, own, depth)
    )
    for copy in w_copies[4:]:
        copy.start()
    for i, wide_buf in ((1, kwide), (2, vwide)):
        w_copies[i].wait()
        wide_buf[:, pl.ds(halo, own)] = (
            dot(own_normed, w[i]).astype(jnp.bfloat16).reshape(views, own, depth)
        )
    w_copies[3].wait()

    def mid_copy(v, target, slot):
        return pltpu.make_async_remote_copy(
            src_ref=mid.at[v, lax.rem(target, 2)], dst_ref=held.at[slot, v],
            send_sem=ms.at[target, v], recv_sem=mr.at[slot, v],
            device_id={"view": target}, device_id_type=pl.DeviceIdType.MESH,
        )

    masks = head_masks(own)

    def spatial(batch_views):
        for v in batch_views:
            for k, (dz, dx) in enumerate(DIRECTIONS):

                @pl.when(there(-dz, -dx))
                def _():
                    halo_copy(k, v).wait_recv()

        around = [part for v in batch_views for part in (wide[v, :halo], wide[v, halo + own :])]
        tokens = rms_norm(jnp.concatenate(around, axis=0), gain)
        outer = wide.shape[1] - own
        for i, wide_buf in ((1, kwide), (2, vwide)):
            product = dot(tokens, w[i]).astype(jnp.bfloat16)
            for n, v in enumerate(batch_views):
                wide_buf[v, :halo] = product[n * outer : n * outer + halo]
                wide_buf[v, halo + own :] = product[n * outer + halo : (n + 1) * outer]
        for v in batch_views:
            parts = []
            for g in range(groups):
                lanes = slice(g * LANES, (g + 1) * LANES)
                parts.append(
                    attend(qbuf[v, :, lanes], kwide[v, :, lanes], vwide[v, :, lanes], bias, masks)
                    .astype(jnp.bfloat16)
                )
            product = dot(jnp.concatenate(parts, axis=1), w[3])
            added = wide[v, pl.ds(halo, own)].astype(jnp.float32) + product
            mid[v] = added.astype(jnp.bfloat16).reshape(2, share, depth)
            for j in range(nv - 1):
                mid_copy(v, peer(j), me).start()
            held[me, v] = mid[v, core]

    gain_time = gain_rows[:, depth:]

    def cut(array, h):
        part = array.reshape(-1, share, array.shape[-1])[:, h * COLS : (h + 1) * COLS]
        return part.reshape(-1, array.shape[-1])

    def temporal(batch_views):
        batch = len(batch_views)
        for v in batch_views:
            for j in range(nv - 1):
                mid_copy(v, peer(j), peer(j)).wait_recv()
        tokens = jnp.concatenate(
            [held[:, v].reshape(nv * share, depth) for v in batch_views], axis=0
        )
        tokens = rms_norm(tokens, gain_time)
        normed[:batch] = tokens.reshape(batch, nv, share, depth)
        for i, buf in ((5, kbuf), (6, vbuf)):
            product = dot(tokens, w[i])
            for n, v in enumerate(batch_views):
                rows = product[n * nv * share : (n + 1) * nv * share]
                for h in range(cuts):
                    buf[h, v] = cut(rows, h).astype(jnp.bfloat16)
        mine = normed[:batch, pl.ds(chip * 2, 2)].reshape(batch * 2 * share, depth)
        queries = dot(mine, w[4]).astype(jnp.bfloat16).astype(jnp.float32) * scale
        queries = queries.reshape(batch, 2, cuts, COLS, depth)
        for n, v in enumerate(batch_views):
            for c in range(2):
                for h in range(cuts):
                    qcut[c, h, v] = queries[n, c, h]

    def turn(v, carry):
        spatial([v])
        return carry

    lax.fori_loop(0, views, turn, 0)
    for i in range(4, 8):
        w_copies[i].wait()
    if views > 1:
        temporal(list(range(views - 1)))
    temporal([views - 1])

    back_copy = pltpu.make_async_remote_copy(
        src_ref=back, dst_ref=out_ref.at[:, core], send_sem=bs, recv_sem=br,
        device_id={"view": beside}, device_id_type=pl.DeviceIdType.MESH,
    )
    shape = (views * COLS, nv * views * COLS)
    query = lax.broadcasted_iota(jnp.int32, shape, 0)
    key = lax.broadcasted_iota(jnp.int32, shape, 1)
    same = jnp.where(lax.rem(query, COLS) == lax.rem(key, COLS), 0.0, very_negative)
    same = same.astype(jnp.float32)
    masks = head_masks(shape[0])
    for source_core in (1 - core, core):
        cut_parts = []
        for h in range(cuts):
            query_cut = qcut[source_core, h].reshape(shape[0], depth).astype(jnp.bfloat16)
            key_cut = kbuf[h].reshape(shape[1], depth)
            value_cut = vbuf[h].reshape(shape[1], depth)
            parts = []
            for g in range(groups):
                lanes = slice(g * LANES, (g + 1) * LANES)
                parts.append(
                    attend(query_cut[:, lanes], key_cut[:, lanes], value_cut[:, lanes], same, masks)
                )
            cut_parts.append(jnp.concatenate(parts, axis=1).reshape(views, COLS, depth))
        attended = jnp.concatenate(cut_parts, axis=1).reshape(views * share, depth)
        product = dot(attended.astype(jnp.bfloat16), w[7])
        middle = held[chip * 2 + source_core].reshape(views * share, depth)
        refined = (middle.astype(jnp.float32) + product).astype(jnp.bfloat16)
        refined = refined.reshape(views, share, depth)
        if source_core is core:
            out_ref[:, core] = refined
        else:
            back[...] = refined
            back_copy.start()

    back_copy.wait()
    for j in range(nv - 1):
        for v in range(views):
            mid_copy(v, peer(j), me).wait_send()
    for v in range(views):
        for k, (dz, dx) in enumerate(DIRECTIONS):

            @pl.when(there(dz, dx))
            def _():
                halo_copy(k, v).wait_send()


def body(sizes, view_maps, gain_spatial, *rest):
    spatial, gain_temporal, temporal = rest[:4], rest[4], rest[5:]
    views, height, width, depth = view_maps.shape
    nv = sizes[0]
    own = height * width
    share = own // 2
    cuts = share // COLS
    side_rows = -(-RADIUS * height // ROWS) * ROWS
    wide = own + 2 * RADIUS * width + 6 * side_rows
    assert nv % 2 == 0 and own % 2 == 0 and share % ROWS == 0 and width % ROWS == 0
    assert height >= RADIUS and width >= RADIUS and depth % LANES == 0
    half = jnp.bfloat16
    hbm = pl.BlockSpec(memory_space=pltpu.HBM)
    vmem = pl.BlockSpec(memory_space=pltpu.VMEM)
    dma = pltpu.SemaphoreType.DMA
    products = 2 * depth * depth * (8 * views * own + 2 * views * (wide - own))
    result = pl.pallas_call(
        functools.partial(kernel, height, width, side_rows, sizes),
        out_shape=jax.ShapeDtypeStruct((views, 2, share, depth), half),
        in_specs=[hbm] * 10,
        out_specs=vmem,
        scratch_shapes=[
            pltpu.VMEM((views, wide, depth), half),
            pltpu.VMEM((views, 2, side_rows, depth), half),
            pltpu.VMEM((8, depth, depth), half),
            pltpu.VMEM((views, own, depth), half),
            pltpu.VMEM((views, 2, share, depth), half),
            pltpu.VMEM((nv, views, share, depth), half),
            pltpu.VMEM((max(1, views - 1), nv, share, depth), half),
            pltpu.VMEM((cuts, views, nv * COLS, depth), half),
            pltpu.VMEM((cuts, views, nv * COLS, depth), half),
            pltpu.VMEM((2, cuts, views, COLS, depth), jnp.float32),
            pltpu.VMEM((views, share, depth), half),
            pltpu.VMEM((views, wide, depth), half),
            pltpu.VMEM((views, wide, depth), half),
            pltpu.VMEM((2 * depth,), jnp.float32),
            dma(()),
            dma((8,)),
            dma((len(DIRECTIONS), views)),
            dma((len(DIRECTIONS), views)),
            dma((nv, views)),
            dma((nv, views)),
            dma(()),
            dma(()),
            dma(()),
        ],
        compiler_params=pltpu.CompilerParams(
            collective_id=0, has_side_effects=True, vmem_limit_bytes=107 * 512 * 1024
        ),
        cost_estimate=pl.CostEstimate(
            flops=products, bytes_accessed=16 * depth * depth, transcendentals=0
        ),
    )(
        view_maps.reshape(views, own, depth),
        jnp.concatenate([gain_spatial, gain_temporal]),
        *spatial,
        *temporal,
    )
    return result.reshape(view_maps.shape)


def solution(mesh):
    sizes = (mesh.shape["view"], mesh.shape["row"], mesh.shape["col"])
    maps = P("view", "row", "col", None)
    return jax.shard_map(
        functools.partial(body, sizes),
        mesh=mesh,
        in_specs=(maps,) + (P(),) * 10,
        out_specs=maps,
        check_vma=False,
    )
```

```python
import functools

import jax
import jax.numpy as jnp
from jax import lax
from jax.experimental import pallas as pl
from jax.experimental.pallas import tpu as pltpu
from jax.sharding import PartitionSpec as P

HEAD_DIM = 64
RADIUS = 3
LANES = 128
ROWS = 16
COLS = 8

epsilon = 1e-06
very_negative = -1e30
DIRECTIONS = [(dz, dx) for dz in (-1, 0, 1) for dx in (-1, 0, 1) if dz or dx]


def rms_norm(tokens, gain):
    values = tokens.astype(jnp.float32)
    mean = jnp.mean(values * values, axis=-1, keepdims=True)
    return (values * lax.rsqrt(mean + epsilon) * gain).astype(jnp.bfloat16)


def dot(a, b):
    return jnp.dot(a, b, preferred_element_type=jnp.float32)


def dot_t(a, b):
    return lax.dot_general(a, b, (((1,), (1,)), ((), ())), preferred_element_type=jnp.float32)


def first_head(rows):
    return lax.broadcasted_iota(jnp.int32, (rows, LANES), 1) < HEAD_DIM


def attend(stacked, key, value, bias):
    rows = bias.shape[0]
    scores = dot_t(stacked, key)
    scores = (scores.reshape(2, rows, -1) + bias[None]).reshape(2 * rows, -1)
    weights = jnp.exp(scores - jnp.max(scores, axis=-1, keepdims=True)).astype(jnp.bfloat16)
    mixed = dot(weights, jnp.concatenate([value, jnp.ones_like(value)], axis=1))
    head = first_head(rows)
    total = jnp.where(head, mixed[:rows, LANES:], mixed[rows:, LANES:])
    return jnp.where(head, mixed[:rows, :LANES], mixed[rows:, :LANES]) / total


def kernel(
    height, width, side_rows, sizes, x_hbm, gains_hbm, *refs
):
    nv, nz, nx = sizes
    weights_hbm, refs = refs[:8], refs[8:]
    out_ref, wide, sides, w, qbuf, mid, held, normed, kbuf, vbuf, qcut, back, kwide, vwide, gains = refs[:15]
    x_sem, w_sem, hs, hr, ms, mr, bs, br, g_sem = refs[15:]
    views, own, depth = x_hbm.shape
    share = own // 2
    cuts = share // COLS
    halo = RADIUS * width
    main = own + 2 * halo
    me, z, x = lax.axis_index("view"), lax.axis_index("row"), lax.axis_index("col")

    x_copy = pltpu.make_async_copy(x_hbm, wide.at[:, pl.ds(halo, own)], x_sem)
    x_copy.start()
    gain_copy = pltpu.make_async_copy(gains_hbm, gains, g_sem)
    gain_copy.start()
    w_copies = [
        pltpu.make_async_copy(weights_hbm[i], w.at[i], w_sem.at[i]) for i in range(8)
    ]
    for copy in w_copies[:4]:
        copy.start()

    def there(dz, dx):
        ok = None
        for place, step, count in ((z, dz, nz), (x, dx, nx)):
            if step:
                one = place > 0 if step < 0 else place < count - 1
                ok = one if ok is None else ok & one
        return ok

    chip, core = me // 2, lax.rem(me, 2)
    beside = chip * 2 + 1 - core

    def peer(j):
        if j == nv - 2:
            return beside
        there = lax.rem(chip + j // 2 + 1, nv // 2)
        return there * 2 + (core if j % 2 == 0 else 1 - core)

    wide[:, :halo] = jnp.zeros((views, halo, depth), wide.dtype)
    wide[:, halo + own :] = jnp.zeros((views, wide.shape[1] - halo - own, depth), wide.dtype)

    barrier = pltpu.get_barrier_semaphore()
    expected = jnp.int32(nv - 1)
    for dz, dx in DIRECTIONS:
        ok = there(dz, dx)
        expected = expected + ok.astype(jnp.int32)

        @pl.when(ok)
        def _():
            pl.semaphore_signal(
                barrier, inc=1, device_id={"row": z + dz, "col": x + dx},
                device_id_type=pl.DeviceIdType.MESH,
            )

    for j in range(nv - 1):
        pl.semaphore_signal(
            barrier, inc=1, device_id={"view": peer(j)}, device_id_type=pl.DeviceIdType.MESH
        )

    pl.semaphore_wait(barrier, expected)

    def halo_copy(k, v):
        dz, dx = DIRECTIONS[k]
        if dx == 0:
            start = own - halo if dz > 0 else 0
            source = x_hbm.at[v, pl.ds(start, halo)]
            target = wide.at[v, pl.ds(0 if dz > 0 else halo + own, halo)]
        else:
            source = sides.at[v, 0 if dx < 0 else 1]
            block = (0 if dx > 0 else 3) + 1 - dz
            target = wide.at[v, pl.ds(main + block * side_rows, side_rows)]
        return pltpu.make_async_remote_copy(
            src_ref=source, dst_ref=target, send_sem=hs.at[k, v], recv_sem=hr.at[k, v],
            device_id={"row": z + dz, "col": x + dx}, device_id_type=pl.DeviceIdType.MESH,
        )

    def send(v, wanted):
        for k, (dz, dx) in enumerate(DIRECTIONS):
            if wanted(dx):

                @pl.when(there(dz, dx))
                def _():
                    halo_copy(k, v).start()

    early = min(2, views)
    for v in range(early):
        send(v, lambda dx: dx == 0)
    x_copy.wait()
    row = lax.broadcasted_iota(jnp.int32, (2 * side_rows, own), 0)
    cell = lax.broadcasted_iota(jnp.int32, (2 * side_rows, own), 1)
    right = row >= side_rows
    t = jnp.where(right, row - side_rows, row)
    wanted = (t // RADIUS) * width + lax.rem(t, RADIUS) + jnp.where(right, width - RADIUS, 0)
    pick = ((cell == wanted) & (t < RADIUS * height)).astype(jnp.bfloat16)
    for v in range(views):
        packed = dot(pick, wide[v, pl.ds(halo, own)]).astype(jnp.bfloat16)
        sides[v] = packed.reshape(2, side_rows, depth)
        if v >= early:
            send(v, lambda dx: dx == 0)
        send(v, lambda dx: dx != 0)

    shape = (own, wide.shape[1])
    query = lax.broadcasted_iota(jnp.int32, shape, 0)
    key = lax.broadcasted_iota(jnp.int32, shape, 1)
    query_row, query_col = query // width, lax.rem(query, width)
    at_side = key >= main
    side_key = key - main
    block, t = side_key // side_rows, lax.rem(side_key, side_rows)
    vertical, on_right = lax.rem(block, 3), block // 3
    key_row = jnp.where(at_side, (vertical - 1) * height + t // RADIUS, key // width - RADIUS)
    key_col = jnp.where(
        at_side, jnp.where(on_right > 0, width, -RADIUS) + lax.rem(t, RADIUS), lax.rem(key, width)
    )
    map_row, map_col = z * height + key_row, x * width + key_col
    seen = (
        (jnp.abs(key_row - query_row) <= RADIUS)
        & (jnp.abs(key_col - query_col) <= RADIUS)
        & (map_row >= 0) & (map_row < nz * height)
        & (map_col >= 0) & (map_col < nx * width)
        & (jnp.logical_not(at_side) | (t < RADIUS * height))
    )
    bias = jnp.where(seen, 0.0, very_negative).astype(jnp.float32)
    scale = HEAD_DIM ** -0.5
    gain_copy.wait()
    gain_rows = gains[...].reshape(1, 2 * depth)
    gain = gain_rows[:, :depth]
    groups = depth // LANES

    own_normed = rms_norm(wide[:, pl.ds(halo, own)].reshape(views * own, depth), gain)
    w_copies[0].wait()
    queries = dot(own_normed, w[0]).astype(jnp.bfloat16).astype(jnp.float32) * scale
    head = first_head(views * own)
    for g in range(groups):
        pair = queries[:, g * LANES : (g + 1) * LANES]
        for n, kept in enumerate((jnp.where(head, pair, 0.0), jnp.where(head, 0.0, pair))):
            qbuf[:, g, n * own : (n + 1) * own] = (
                kept.astype(jnp.bfloat16).reshape(views, own, LANES)
            )
    for copy in w_copies[4:]:
        copy.start()
    for i, wide_buf in ((1, kwide), (2, vwide)):
        w_copies[i].wait()
        wide_buf[:, pl.ds(halo, own)] = (
            dot(own_normed, w[i]).astype(jnp.bfloat16).reshape(views, own, depth)
        )
    w_copies[3].wait()

    def mid_copy(v, target, slot):
        return pltpu.make_async_remote_copy(
            src_ref=mid.at[v, lax.rem(target, 2)], dst_ref=held.at[slot, v],
            send_sem=ms.at[target, v], recv_sem=mr.at[slot, v],
            device_id={"view": target}, device_id_type=pl.DeviceIdType.MESH,
        )


    def spatial(batch_views):
        for v in batch_views:
            for k, (dz, dx) in enumerate(DIRECTIONS):

                @pl.when(there(-dz, -dx))
                def _():
                    halo_copy(k, v).wait_recv()

        around = [part for v in batch_views for part in (wide[v, :halo], wide[v, halo + own :])]
        tokens = rms_norm(jnp.concatenate(around, axis=0), gain)
        outer = wide.shape[1] - own
        for i, wide_buf in ((1, kwide), (2, vwide)):
            product = dot(tokens, w[i]).astype(jnp.bfloat16)
            for n, v in enumerate(batch_views):
                wide_buf[v, :halo] = product[n * outer : n * outer + halo]
                wide_buf[v, halo + own :] = product[n * outer + halo : (n + 1) * outer]
        for v in batch_views:
            parts = []
            for g in range(groups):
                lanes = slice(g * LANES, (g + 1) * LANES)
                parts.append(
                    attend(qbuf[v, g], kwide[v, :, lanes], vwide[v, :, lanes], bias)
                    .astype(jnp.bfloat16)
                )
            product = dot(jnp.concatenate(parts, axis=1), w[3])
            added = wide[v, pl.ds(halo, own)].astype(jnp.float32) + product
            mid[v] = added.astype(jnp.bfloat16).reshape(2, share, depth)
            for j in range(nv - 1):
                mid_copy(v, peer(j), me).start()
            held[me, v] = mid[v, core]

    gain_time = gain_rows[:, depth:]

    def cut(array, h):
        part = array.reshape(-1, share, array.shape[-1])[:, h * COLS : (h + 1) * COLS]
        return part.reshape(-1, array.shape[-1])

    def temporal(batch_views):
        batch = len(batch_views)
        for v in batch_views:
            for j in range(nv - 1):
                mid_copy(v, peer(j), peer(j)).wait_recv()
        tokens = jnp.concatenate(
            [held[:, v].reshape(nv * share, depth) for v in batch_views], axis=0
        )
        tokens = rms_norm(tokens, gain_time)
        normed[:batch] = tokens.reshape(batch, nv, share, depth)
        for i, buf in ((5, kbuf), (6, vbuf)):
            product = dot(tokens, w[i])
            for n, v in enumerate(batch_views):
                rows = product[n * nv * share : (n + 1) * nv * share]
                for h in range(cuts):
                    buf[h, v] = cut(rows, h).astype(jnp.bfloat16)
        mine = normed[:batch, pl.ds(chip * 2, 2)].reshape(batch * 2 * share, depth)
        queries = dot(mine, w[4]).astype(jnp.bfloat16).astype(jnp.float32) * scale
        queries = queries.reshape(batch, 2, cuts, COLS, depth)
        for n, v in enumerate(batch_views):
            for c in range(2):
                for h in range(cuts):
                    qcut[h, c, v] = queries[n, c, h]

    def turn(v, carry):
        spatial([v])
        return carry

    lax.fori_loop(0, views, turn, 0)
    for i in range(4, 8):
        w_copies[i].wait()
    if views > 1:
        temporal(list(range(views - 1)))
    temporal([views - 1])

    def back_copy(c):
        return pltpu.make_async_remote_copy(
            src_ref=back.at[c, 1 - core], dst_ref=out_ref.at[:, core, pl.ds(c * ROWS, ROWS)],
            send_sem=bs.at[c], recv_sem=br.at[c],
            device_id={"view": beside}, device_id_type=pl.DeviceIdType.MESH,
        )

    shape = (2 * views * COLS, nv * views * COLS)
    query = lax.broadcasted_iota(jnp.int32, shape, 0)
    key = lax.broadcasted_iota(jnp.int32, shape, 1)
    same = jnp.where(lax.rem(query, COLS) == lax.rem(key, COLS), 0.0, very_negative)
    same = same.astype(jnp.float32)
    head = first_head(shape[0])
    for c in range(share // ROWS):
        cut_parts = []
        for h in range(c * ROWS // COLS, (c + 1) * ROWS // COLS):
            parts = []
            for g in range(groups):
                lanes = slice(g * LANES, (g + 1) * LANES)
                pair = qcut[h, :, :, :, lanes].reshape(shape[0], LANES)
                stacked = jnp.concatenate(
                    [jnp.where(head, pair, 0.0), jnp.where(head, 0.0, pair)], axis=0
                ).astype(jnp.bfloat16)
                key_cut = kbuf[h, :, :, lanes].reshape(shape[1], LANES)
                value_cut = vbuf[h, :, :, lanes].reshape(shape[1], LANES)
                parts.append(attend(stacked, key_cut, value_cut, same))
            cut_parts.append(jnp.concatenate(parts, axis=1).reshape(2 * views, COLS, depth))
        attended = jnp.concatenate(cut_parts, axis=1).reshape(2 * views * ROWS, depth)
        product = dot(attended.astype(jnp.bfloat16), w[7])
        middle = held[pl.ds(chip * 2, 2), :, c * ROWS : (c + 1) * ROWS]
        refined = middle.reshape(2 * views * ROWS, depth).astype(jnp.float32) + product
        back[c] = refined.astype(jnp.bfloat16).reshape(2, views, ROWS, depth)
        back_copy(c).start()
        out_ref[:, core, c * ROWS : (c + 1) * ROWS] = back[c, core]

    for c in range(share // ROWS):
        back_copy(c).wait()
    for j in range(nv - 1):
        for v in range(views):
            mid_copy(v, peer(j), me).wait_send()
    for v in range(views):
        for k, (dz, dx) in enumerate(DIRECTIONS):

            @pl.when(there(dz, dx))
            def _():
                halo_copy(k, v).wait_send()


def body(sizes, view_maps, gain_spatial, *rest):
    spatial, gain_temporal, temporal = rest[:4], rest[4], rest[5:]
    views, height, width, depth = view_maps.shape
    nv = sizes[0]
    own = height * width
    share = own // 2
    cuts = share // COLS
    side_rows = -(-RADIUS * height // ROWS) * ROWS
    wide = own + 2 * RADIUS * width + 6 * side_rows
    assert nv % 2 == 0 and own % 2 == 0 and share % ROWS == 0 and width % ROWS == 0
    assert height >= RADIUS and width >= RADIUS and depth % LANES == 0
    half = jnp.bfloat16
    hbm = pl.BlockSpec(memory_space=pltpu.HBM)
    vmem = pl.BlockSpec(memory_space=pltpu.VMEM)
    dma = pltpu.SemaphoreType.DMA
    products = 2 * depth * depth * (8 * views * own + 2 * views * (wide - own))
    result = pl.pallas_call(
        functools.partial(kernel, height, width, side_rows, sizes),
        out_shape=jax.ShapeDtypeStruct((views, 2, share, depth), half),
        in_specs=[hbm] * 10,
        out_specs=vmem,
        scratch_shapes=[
            pltpu.VMEM((views, wide, depth), half),
            pltpu.VMEM((views, 2, side_rows, depth), half),
            pltpu.VMEM((8, depth, depth), half),
            pltpu.VMEM((views, depth // LANES, 2 * own, LANES), half),
            pltpu.VMEM((views, 2, share, depth), half),
            pltpu.VMEM((nv, views, share, depth), half),
            pltpu.VMEM((max(1, views - 1), nv, share, depth), half),
            pltpu.VMEM((cuts, views, nv * COLS, depth), half),
            pltpu.VMEM((cuts, views, nv * COLS, depth), half),
            pltpu.VMEM((cuts, 2, views, COLS, depth), jnp.float32),
            pltpu.VMEM((share // ROWS, 2, views, ROWS, depth), half),
            pltpu.VMEM((views, wide, depth), half),
            pltpu.VMEM((views, wide, depth), half),
            pltpu.VMEM((2 * depth,), jnp.float32),
            dma(()),
            dma((8,)),
            dma((len(DIRECTIONS), views)),
            dma((len(DIRECTIONS), views)),
            dma((nv, views)),
            dma((nv, views)),
            dma((share // ROWS,)),
            dma((share // ROWS,)),
            dma(()),
        ],
        compiler_params=pltpu.CompilerParams(
            collective_id=0, has_side_effects=True, vmem_limit_bytes=107 * 512 * 1024
        ),
        cost_estimate=pl.CostEstimate(
            flops=products, bytes_accessed=16 * depth * depth, transcendentals=0
        ),
    )(
        view_maps.reshape(views, own, depth),
        jnp.concatenate([gain_spatial, gain_temporal]),
        *spatial,
        *temporal,
    )
    return result.reshape(view_maps.shape)


def solution(mesh):
    sizes = (mesh.shape["view"], mesh.shape["row"], mesh.shape["col"])
    maps = P("view", "row", "col", None)
    return jax.shard_map(
        functools.partial(body, sizes),
        mesh=mesh,
        in_specs=(maps,) + (P(),) * 10,
        out_specs=maps,
        check_vma=False,
    )
```

```python
import functools

import jax
import jax.numpy as jnp
from jax import lax
from jax.experimental import pallas as pl
from jax.experimental.pallas import tpu as pltpu
from jax.sharding import PartitionSpec as P

HEAD_DIM = 64
RADIUS = 3
LANES = 128
ROWS = 16
COLS = 8

epsilon = 1e-06
very_negative = -1e30
DIRECTIONS = [(dz, dx) for dz in (-1, 0, 1) for dx in (-1, 0, 1) if dz or dx]


def rms_norm(tokens, gain):
    values = tokens.astype(jnp.float32)
    mean = jnp.mean(values * values, axis=-1, keepdims=True)
    return (values * lax.rsqrt(mean + epsilon) * gain).astype(jnp.bfloat16)


def dot(a, b):
    return jnp.dot(a, b, preferred_element_type=jnp.float32)


def dot_t(a, b):
    return lax.dot_general(a, b, (((1,), (1,)), ((), ())), preferred_element_type=jnp.float32)


def first_head(rows):
    return lax.broadcasted_iota(jnp.int32, (rows, LANES), 1) < HEAD_DIM


def attend(stacked, key, value, bias):
    rows = bias.shape[0]
    scores = dot_t(stacked, key)
    scores = (scores.reshape(2, rows, -1) + bias[None]).reshape(2 * rows, -1)
    weights = jnp.exp(scores - jnp.max(scores, axis=-1, keepdims=True)).astype(jnp.bfloat16)
    mixed = dot(weights, jnp.concatenate([value, jnp.ones_like(value)], axis=1))
    head = first_head(rows)
    total = jnp.where(head, mixed[:rows, LANES:], mixed[rows:, LANES:])
    return jnp.where(head, mixed[:rows, :LANES], mixed[rows:, :LANES]) / total


def kernel(
    height, width, side_rows, sizes, x_hbm, gains_hbm, *refs
):
    nv, nz, nx = sizes
    weights_hbm, refs = refs[:8], refs[8:]
    out_ref, wide, sides, w, qbuf, mid, held, normed, kbuf, vbuf, qcut, back, kwide, vwide, gains = refs[:15]
    x_sem, w_sem, hs, hr, ms, mr, bs, br, g_sem = refs[15:]
    views, own, depth = x_hbm.shape
    share = own // 2
    cuts = share // COLS
    halo = RADIUS * width
    main = own + 2 * halo
    me, z, x = lax.axis_index("view"), lax.axis_index("row"), lax.axis_index("col")

    x_copy = pltpu.make_async_copy(x_hbm, wide.at[:, pl.ds(halo, own)], x_sem)
    x_copy.start()
    gain_copy = pltpu.make_async_copy(gains_hbm, gains, g_sem)
    gain_copy.start()
    w_copies = [
        pltpu.make_async_copy(weights_hbm[i], w.at[i], w_sem.at[i]) for i in range(8)
    ]
    for copy in w_copies[:4]:
        copy.start()

    def there(dz, dx):
        ok = None
        for place, step, count in ((z, dz, nz), (x, dx, nx)):
            if step:
                one = place > 0 if step < 0 else place < count - 1
                ok = one if ok is None else ok & one
        return ok

    chip, core = me // 2, lax.rem(me, 2)
    beside = chip * 2 + 1 - core

    def peer(j):
        if j == nv - 2:
            return beside
        there = lax.rem(chip + j // 2 + 1, nv // 2)
        return there * 2 + (core if j % 2 == 0 else 1 - core)

    wide[:, :halo] = jnp.zeros((views, halo, depth), wide.dtype)
    wide[:, halo + own :] = jnp.zeros((views, wide.shape[1] - halo - own, depth), wide.dtype)

    barrier = pltpu.get_barrier_semaphore()
    expected = jnp.int32(nv - 1)
    for dz, dx in DIRECTIONS:
        ok = there(dz, dx)
        expected = expected + ok.astype(jnp.int32)

        @pl.when(ok)
        def _():
            pl.semaphore_signal(
                barrier, inc=1, device_id={"row": z + dz, "col": x + dx},
                device_id_type=pl.DeviceIdType.MESH,
            )

    for j in range(nv - 1):
        pl.semaphore_signal(
            barrier, inc=1, device_id={"view": peer(j)}, device_id_type=pl.DeviceIdType.MESH
        )

    pl.semaphore_wait(barrier, expected)

    def halo_copy(k, v):
        dz, dx = DIRECTIONS[k]
        if dx == 0:
            start = own - halo if dz > 0 else 0
            source = x_hbm.at[v, pl.ds(start, halo)]
            target = wide.at[v, pl.ds(0 if dz > 0 else halo + own, halo)]
        else:
            source = sides.at[v, 0 if dx < 0 else 1]
            block = (0 if dx > 0 else 3) + 1 - dz
            target = wide.at[v, pl.ds(main + block * side_rows, side_rows)]
        return pltpu.make_async_remote_copy(
            src_ref=source, dst_ref=target, send_sem=hs.at[k, v], recv_sem=hr.at[k, v],
            device_id={"row": z + dz, "col": x + dx}, device_id_type=pl.DeviceIdType.MESH,
        )

    def send(v, wanted):
        for k, (dz, dx) in enumerate(DIRECTIONS):
            if wanted(dx):

                @pl.when(there(dz, dx))
                def _():
                    halo_copy(k, v).start()

    early = min(2, views)
    for v in range(early):
        send(v, lambda dx: dx == 0)
    x_copy.wait()
    row = lax.broadcasted_iota(jnp.int32, (2 * side_rows, own), 0)
    cell = lax.broadcasted_iota(jnp.int32, (2 * side_rows, own), 1)
    right = row >= side_rows
    t = jnp.where(right, row - side_rows, row)
    wanted = (t // RADIUS) * width + lax.rem(t, RADIUS) + jnp.where(right, width - RADIUS, 0)
    pick = ((cell == wanted) & (t < RADIUS * height)).astype(jnp.bfloat16)
    for v in range(views):
        packed = dot(pick, wide[v, pl.ds(halo, own)]).astype(jnp.bfloat16)
        sides[v] = packed.reshape(2, side_rows, depth)
        if v >= early:
            send(v, lambda dx: dx == 0)
        send(v, lambda dx: dx != 0)

    shape = (own, wide.shape[1])
    query = lax.broadcasted_iota(jnp.int32, shape, 0)
    key = lax.broadcasted_iota(jnp.int32, shape, 1)
    query_row, query_col = query // width, lax.rem(query, width)
    at_side = key >= main
    side_key = key - main
    block, t = side_key // side_rows, lax.rem(side_key, side_rows)
    vertical, on_right = lax.rem(block, 3), block // 3
    key_row = jnp.where(at_side, (vertical - 1) * height + t // RADIUS, key // width - RADIUS)
    key_col = jnp.where(
        at_side, jnp.where(on_right > 0, width, -RADIUS) + lax.rem(t, RADIUS), lax.rem(key, width)
    )
    map_row, map_col = z * height + key_row, x * width + key_col
    seen = (
        (jnp.abs(key_row - query_row) <= RADIUS)
        & (jnp.abs(key_col - query_col) <= RADIUS)
        & (map_row >= 0) & (map_row < nz * height)
        & (map_col >= 0) & (map_col < nx * width)
        & (jnp.logical_not(at_side) | (t < RADIUS * height))
    )
    bias = jnp.where(seen, 0.0, very_negative).astype(jnp.float32)
    scale = HEAD_DIM ** -0.5
    gain_copy.wait()
    gain_rows = gains[...].reshape(1, 2 * depth)
    gain = gain_rows[:, :depth]
    groups = depth // LANES

    own_normed = rms_norm(wide[:, pl.ds(halo, own)].reshape(views * own, depth), gain)
    w_copies[0].wait()
    queries = dot(own_normed, w[0]).astype(jnp.bfloat16).astype(jnp.float32) * scale
    head = first_head(views * own)
    for g in range(groups):
        pair = queries[:, g * LANES : (g + 1) * LANES]
        for n, kept in enumerate((jnp.where(head, pair, 0.0), jnp.where(head, 0.0, pair))):
            qbuf[:, g, n * own : (n + 1) * own] = (
                kept.astype(jnp.bfloat16).reshape(views, own, LANES)
            )
    for copy in w_copies[4:]:
        copy.start()
    for i, wide_buf in ((1, kwide), (2, vwide)):
        w_copies[i].wait()
        wide_buf[:, pl.ds(halo, own)] = (
            dot(own_normed, w[i]).astype(jnp.bfloat16).reshape(views, own, depth)
        )
    w_copies[3].wait()

    def mid_copy(v, target, slot):
        return pltpu.make_async_remote_copy(
            src_ref=mid.at[v, lax.rem(target, 2)], dst_ref=held.at[slot, v],
            send_sem=ms.at[target, v], recv_sem=mr.at[slot, v],
            device_id={"view": target}, device_id_type=pl.DeviceIdType.MESH,
        )


    def spatial(batch_views):
        for v in batch_views:
            for k, (dz, dx) in enumerate(DIRECTIONS):

                @pl.when(there(-dz, -dx))
                def _():
                    halo_copy(k, v).wait_recv()

        around = [part for v in batch_views for part in (wide[v, :halo], wide[v, halo + own :])]
        tokens = rms_norm(jnp.concatenate(around, axis=0), gain)
        outer = wide.shape[1] - own
        for i, wide_buf in ((1, kwide), (2, vwide)):
            product = dot(tokens, w[i]).astype(jnp.bfloat16)
            for n, v in enumerate(batch_views):
                wide_buf[v, :halo] = product[n * outer : n * outer + halo]
                wide_buf[v, halo + own :] = product[n * outer + halo : (n + 1) * outer]
        for v in batch_views:
            parts = []
            for g in range(groups):
                lanes = slice(g * LANES, (g + 1) * LANES)
                parts.append(
                    attend(qbuf[v, g], kwide[v, :, lanes], vwide[v, :, lanes], bias)
                    .astype(jnp.bfloat16)
                )
            product = dot(jnp.concatenate(parts, axis=1), w[3])
            added = wide[v, pl.ds(halo, own)].astype(jnp.float32) + product
            mid[v] = added.astype(jnp.bfloat16).reshape(2, share, depth)
            for j in range(nv - 1):
                mid_copy(v, peer(j), me).start()
            held[me, v] = mid[v, core]

    gain_time = gain_rows[:, depth:]

    def cut(array, h):
        part = array.reshape(-1, share, array.shape[-1])[:, h * COLS : (h + 1) * COLS]
        return part.reshape(-1, array.shape[-1])

    def temporal(batch_views):
        batch = len(batch_views)
        for v in batch_views:
            for j in range(nv - 1):
                mid_copy(v, peer(j), peer(j)).wait_recv()
        tokens = jnp.concatenate(
            [held[:, v].reshape(nv * share, depth) for v in batch_views], axis=0
        )
        tokens = rms_norm(tokens, gain_time)
        normed[:batch] = tokens.reshape(batch, nv, share, depth)
        for i, buf in ((5, kbuf), (6, vbuf)):
            product = dot(tokens, w[i])
            for n, v in enumerate(batch_views):
                rows = product[n * nv * share : (n + 1) * nv * share]
                for h in range(cuts):
                    buf[h, v] = cut(rows, h).astype(jnp.bfloat16)
        mine = normed[:batch, pl.ds(chip * 2, 2)].reshape(batch * 2 * share, depth)
        queries = dot(mine, w[4]).astype(jnp.bfloat16).astype(jnp.float32) * scale
        queries = queries.reshape(batch, 2, cuts, COLS, depth)
        for n, v in enumerate(batch_views):
            for c in range(2):
                for h in range(cuts):
                    qcut[h, c, v] = queries[n, c, h]

    def turn(v, carry):
        spatial([v])
        return carry

    lax.fori_loop(0, views, turn, 0)
    for i in range(4, 8):
        w_copies[i].wait()
    if views > 1:
        temporal(list(range(views - 1)))
    temporal([views - 1])

    back_copy = pltpu.make_async_remote_copy(
        src_ref=back, dst_ref=out_ref.at[:, core], send_sem=bs, recv_sem=br,
        device_id={"view": beside}, device_id_type=pl.DeviceIdType.MESH,
    )
    shape = (views * COLS, nv * views * COLS)
    query = lax.broadcasted_iota(jnp.int32, shape, 0)
    key = lax.broadcasted_iota(jnp.int32, shape, 1)
    same = jnp.where(lax.rem(query, COLS) == lax.rem(key, COLS), 0.0, very_negative)
    same = same.astype(jnp.float32)
    head = first_head(shape[0])
    for source_core in (1 - core, core):
        cut_parts = []
        for h in range(cuts):
            parts = []
            for g in range(groups):
                lanes = slice(g * LANES, (g + 1) * LANES)
                pair = qcut[h, source_core, :, :, lanes].reshape(shape[0], LANES)
                stacked = jnp.concatenate(
                    [jnp.where(head, pair, 0.0), jnp.where(head, 0.0, pair)], axis=0
                ).astype(jnp.bfloat16)
                key_cut = kbuf[h, :, :, lanes].reshape(shape[1], LANES)
                value_cut = vbuf[h, :, :, lanes].reshape(shape[1], LANES)
                parts.append(attend(stacked, key_cut, value_cut, same))
            cut_parts.append(jnp.concatenate(parts, axis=1).reshape(views, COLS, depth))
        attended = jnp.concatenate(cut_parts, axis=1).reshape(views * share, depth)
        product = dot(attended.astype(jnp.bfloat16), w[7])
        middle = held[chip * 2 + source_core].reshape(views * share, depth)
        refined = (middle.astype(jnp.float32) + product).astype(jnp.bfloat16)
        refined = refined.reshape(views, share, depth)
        if source_core is core:
            out_ref[:, core] = refined
        else:
            back[...] = refined
            back_copy.start()

    back_copy.wait()
    for j in range(nv - 1):
        for v in range(views):
            mid_copy(v, peer(j), me).wait_send()
    for v in range(views):
        for k, (dz, dx) in enumerate(DIRECTIONS):

            @pl.when(there(dz, dx))
            def _():
                halo_copy(k, v).wait_send()


def body(sizes, view_maps, gain_spatial, *rest):
    spatial, gain_temporal, temporal = rest[:4], rest[4], rest[5:]
    views, height, width, depth = view_maps.shape
    nv = sizes[0]
    own = height * width
    share = own // 2
    cuts = share // COLS
    side_rows = -(-RADIUS * height // ROWS) * ROWS
    wide = own + 2 * RADIUS * width + 6 * side_rows
    assert nv % 2 == 0 and own % 2 == 0 and share % ROWS == 0 and width % ROWS == 0
    assert height >= RADIUS and width >= RADIUS and depth % LANES == 0
    half = jnp.bfloat16
    hbm = pl.BlockSpec(memory_space=pltpu.HBM)
    vmem = pl.BlockSpec(memory_space=pltpu.VMEM)
    dma = pltpu.SemaphoreType.DMA
    products = 2 * depth * depth * (8 * views * own + 2 * views * (wide - own))
    result = pl.pallas_call(
        functools.partial(kernel, height, width, side_rows, sizes),
        out_shape=jax.ShapeDtypeStruct((views, 2, share, depth), half),
        in_specs=[hbm] * 10,
        out_specs=vmem,
        scratch_shapes=[
            pltpu.VMEM((views, wide, depth), half),
            pltpu.VMEM((views, 2, side_rows, depth), half),
            pltpu.VMEM((8, depth, depth), half),
            pltpu.VMEM((views, depth // LANES, 2 * own, LANES), half),
            pltpu.VMEM((views, 2, share, depth), half),
            pltpu.VMEM((nv, views, share, depth), half),
            pltpu.VMEM((max(1, views - 1), nv, share, depth), half),
            pltpu.VMEM((cuts, views, nv * COLS, depth), half),
            pltpu.VMEM((cuts, views, nv * COLS, depth), half),
            pltpu.VMEM((cuts, 2, views, COLS, depth), jnp.float32),
            pltpu.VMEM((views, share, depth), half),
            pltpu.VMEM((views, wide, depth), half),
            pltpu.VMEM((views, wide, depth), half),
            pltpu.VMEM((2 * depth,), jnp.float32),
            dma(()),
            dma((8,)),
            dma((len(DIRECTIONS), views)),
            dma((len(DIRECTIONS), views)),
            dma((nv, views)),
            dma((nv, views)),
            dma(()),
            dma(()),
            dma(()),
        ],
        compiler_params=pltpu.CompilerParams(
            collective_id=0, has_side_effects=True, vmem_limit_bytes=107 * 512 * 1024
        ),
        cost_estimate=pl.CostEstimate(
            flops=products, bytes_accessed=16 * depth * depth, transcendentals=0
        ),
    )(
        view_maps.reshape(views, own, depth),
        jnp.concatenate([gain_spatial, gain_temporal]),
        *spatial,
        *temporal,
    )
    return result.reshape(view_maps.shape)


def solution(mesh):
    sizes = (mesh.shape["view"], mesh.shape["row"], mesh.shape["col"])
    maps = P("view", "row", "col", None)
    return jax.shard_map(
        functools.partial(body, sizes),
        mesh=mesh,
        in_specs=(maps,) + (P(),) * 10,
        out_specs=maps,
        check_vma=False,
    )
```
